512 devices in a mesh: sx: 32 (over z, y_hi), sy: 16 (over x, y_lo, core).
Axes of the slice: x: 4, y: 4 (y_hi: 2, y_lo: 2; y = y_hi * 2 + y_lo), z: 16, core: 2. Of those that a mesh axis runs over, the one named last changes fastest.
Arguments:
- volume: bfloat16 [4, 256, 128, 128], P(None, 'sx', 'sy'), may hold values from -6 to 6
- w_first: bfloat16 [16, 4, 3, 3, 3], replicated, may hold values from -0.625 to 0.625
- w_second: bfloat16 [32, 16, 3, 3, 3], replicated, may hold values from -0.3125 to 0.3125
- w_third: bfloat16 [64, 32, 3, 3, 3], P('sy'), may hold values from -0.21875 to 0.21875
- feature_grad: bfloat16 [64, 32, 16, 16], P('sy', 'sx'), may hold values from -48 to 48
Outputs:
- features: bfloat16 [64, 32, 16, 16], P('sy', 'sx')
- first_grad: float32 [16, 4, 3, 3, 3], replicated
- second_grad: float32 [32, 16, 3, 3, 3], replicated
- third_grad: float32 [64, 32, 3, 3, 3], P('sy')
The draws below stay inside these ranges and needn't reach their ends.
All inputs are finite; a program needn't handle non-finite values.
Results may differ from the reference program's by a relative error of at most 0.028.
The reference program's roundings to bfloat16 on the way (of `first_out`, `second_out`, `third_grads`, `second_grads` and `first_grads`) count: a program that leaves them out, or rounds other values in their place, can miss the bound.
Values may be sent and summed in bfloat16 or wider, within the bound.
No kernel may reach another device: no remote copies, remote signals or barrier semaphores. Data moves between devices by JAX's collectives and lax.ppermute only.
A program may use at most 64 MiB of HBM per device.

```python
import math
import jax
import jax.numpy as jnp
from jax import lax

CIN = 4
FA = 16
FB = 32
FC = 64
CD = 8
DEPTH = 256
HEIGHT = 128
WIDTH = 128
N_SX = 32


def block_levels(key, extent, pieces, low, largest):
    factor_of, own = 1.0, jax.random.fold_in(key, 6)
    for axis_at, blocks in pieces:
        heights = jnp.exp(jax.random.uniform(jax.random.fold_in(own, axis_at), (blocks,), jnp.float32, low / len(pieces), largest / len(pieces)))
        factor_of = factor_of * jnp.repeat(heights, extent[axis_at] // blocks).reshape([-1 if axis == axis_at else 1 for axis in range(len(extent))])
    return factor_of


def noise(rng, dims, width, bound, cuts=(), kind=jnp.bfloat16):
    loudness = block_levels(rng, dims, cuts, -0.22, 0.18) if cuts else 1.0
    values = jax.random.normal(rng, dims, jnp.float32) * width * loudness
    return jnp.minimum(jnp.maximum(values, -bound), bound).astype(kind)


def setup_inputs(seed: int = 0) -> dict:
    streams_of = jax.random.split(jax.random.key(seed), 6)
    volume = noise(streams_of[0], (CIN, DEPTH, HEIGHT, WIDTH), 1.0, 6.0, ((1, 32), (2, 16)))
    w_first = noise(streams_of[1], (FA, CIN, 3, 3, 3), (27 * CIN) ** -0.5, 0.625)
    w_second = noise(streams_of[2], (FB, FA, 3, 3, 3), (27 * FA) ** -0.5, 0.3125)
    w_third = noise(streams_of[3], (FC, FB, 3, 3, 3), (27 * FB) ** -0.5, 0.21875, ((0, 16),))
    feature_grad = noise(streams_of[4], (FC, DEPTH // 8, HEIGHT // 8, WIDTH // 8), 8.0, 48.0, ((0, 16), (1, 32)))
    return {"volume": volume, "w_first": w_first, "w_second": w_second, "w_third": w_third, "feature_grad": feature_grad}


SLOPE = 0.3
LAYOUT = ('NCDHW', 'OIDHW', 'NCDHW')

def leaky_relu(values):
    return jnp.where(values > 0, values, SLOPE * values)

def leaky_slope(values):
    return jnp.where(values > 0, 1.0, SLOPE)

def pooled_mean(values):
    chans, depths, rows, cols = values.shape
    shaped = values.reshape(chans, depths // 2, 2, rows // 2, 2, cols // 2, 2)
    return lax.optimization_barrier(jnp.mean(shaped, axis=(2, 4, 6)))

def spread(grads):
    finer = jnp.repeat(jnp.repeat(jnp.repeat(grads, 2, axis=1), 2, axis=2), 2, axis=3)
    return finer * 0.125

def convolve(field, kernels, depth_pad):
    result = lax.conv_general_dilated(field[None], kernels, (1, 1, 1), ((depth_pad, depth_pad), (1, 1), (1, 1)), dimension_numbers=LAYOUT)
    return result[0]

def rounded(values):
    return lax.optimization_barrier(values.astype(jnp.bfloat16)).astype(jnp.float32)

def reference(volume, w_first, w_second, w_third, feature_grad):
    kern_a = w_first.astype(jnp.float32)
    kern_b = w_second.astype(jnp.float32)
    kern_c = w_third.astype(jnp.float32)
    padded = jnp.pad(volume, ((0, 0), (1, 1), (0, 0), (0, 0)))
    block_ids = jnp.arange(N_SX, dtype=jnp.int32)

    def first_slab(index):
        return lax.dynamic_slice_in_dim(padded, index * CD, CD + 2, 1).astype(jnp.float32)

    def first_forward(index):
        return pooled_mean(leaky_relu(convolve(first_slab(index), kern_a, 0))).astype(jnp.bfloat16)
    blocks = lax.map(first_forward, block_ids)
    first_out = jnp.moveaxis(blocks, 0, 1).reshape(FA, DEPTH // 2, HEIGHT // 2, WIDTH // 2)
    first_in = first_out.astype(jnp.float32)
    second_pre = convolve(first_in, kern_b, 1)
    second_out = pooled_mean(leaky_relu(second_pre)).astype(jnp.bfloat16)
    second_in = second_out.astype(jnp.float32)
    third_pre = convolve(second_in, kern_c, 1)
    features = pooled_mean(leaky_relu(third_pre)).astype(jnp.bfloat16)
    third_grads = rounded(leaky_slope(third_pre) * spread(feature_grad.astype(jnp.float32)))
    _, pull_third = jax.vjp(lambda field, kernels: convolve(field, kernels, 1), second_in, kern_c)
    second_up, third_wg = pull_third(third_grads)
    second_grads = rounded(leaky_slope(second_pre) * spread(second_up))
    _, pull_second = jax.vjp(lambda field, kernels: convolve(field, kernels, 1), first_in, kern_b)
    first_up, second_wg = pull_second(second_grads)

    def first_back(summed, index):
        slab = first_slab(index)
        first_pre = convolve(slab, kern_a, 0)
        upper = lax.dynamic_slice_in_dim(first_up, index * (CD // 2), CD // 2, 1)
        first_grads = rounded(leaky_slope(first_pre) * spread(upper))
        _, pull_first = jax.vjp(lambda kernels: convolve(slab, kernels, 0), kern_a)
        return (summed + pull_first(first_grads)[0], None)
    first_wg, _ = lax.scan(first_back, jnp.zeros(kern_a.shape, jnp.float32), block_ids)
    cells = DEPTH * HEIGHT * WIDTH
    first_grad = first_wg * (64.0 / math.sqrt(cells))
    second_grad = second_wg * (8.0 / math.sqrt(cells / 8))
    third_grad = third_wg * (1.0 / math.sqrt(cells / 64))
    return (features, first_grad, second_grad, third_grad)
```

```python
import math

import jax
import jax.numpy as jnp
import numpy as np
from jax import lax
from jax.experimental import pallas as pl
from jax.experimental.pallas import tpu as pltpu
from jax.sharding import PartitionSpec as P

SLOPE = 0.3
BF16 = jnp.bfloat16
F32 = jnp.float32


def tap_shift(rows, cols, out_first, out_rows):
    table = np.zeros((rows, cols, 3, 3, out_rows, cols), np.float32)
    for kh in range(3):
        for kw in range(3):
            for r in range(out_rows):
                for w in range(cols):
                    row, col = out_first + r + kh - 1, w + kw - 1
                    if 0 <= row < rows and 0 <= col < cols:
                        table[row, col, kh, kw, r, w] = 1
    return table.reshape(rows * cols, 9 * out_rows * cols)


def second_spread():
    table = np.zeros((8, 32, 8, 64), np.float32)
    for r in range(8):
        for w in range(64):
            table[2 + r // 2, w // 2, r, w] = 0.125
    return table.reshape(256, 512)


def block_taps():
    table = np.zeros((2, 2, 2, 4, 4, 4, 4, 128), np.float32)
    for pd, ph, pw in np.ndindex(2, 2, 2):
        for kd, kh, kw, c in np.ndindex(3, 3, 3, 4):
            at = ((kd * 3 + kh) * 3 + kw) * 4 + c
            table[pd, ph, pw, kd + pd, kw + pw, kh + ph, c, at] = 1
    return table.reshape(2048, 128)


def dot(a, b):
    return lax.dot_general(a, b, (((1,), (0,)), ((), ())), preferred_element_type=F32)


def dot_t(a, b):
    return lax.dot_general(a, b, (((1,), (1,)), ((), ())), preferred_element_type=F32)


def placed(shape, match, value=1.0, dtype=BF16):
    row, lane = (lax.broadcasted_iota(jnp.int32, shape, axis) for axis in range(2))
    return jnp.where(match(row, lane), value, 0.0).astype(dtype)


def unit(size, dtype):
    return placed((size, size), lambda row, lane: row == lane, 1.0, dtype)


def turned():
    return placed((32, 32), lambda row, lane: lane == (row & 3) * 8 + (row >> 2))


def column_shift(cols):
    def match(row, lane):
        to = (lane & 127) + (lane >> 7) - 1
        return jnp.logical_and(row == to, (row // cols) == (lane & 127) // cols)

    return placed((128, 384), match)


def column_pairs():
    return placed((128, 512), lambda row, lane: row == 2 * (lane & 63) + (lane >> 7) - 1)


def second_pool():
    return placed((512, 128), lambda row, lane: lane == (row >> 7) * 32 + ((row & 63) >> 1), 0.125)


def third_pool():
    def match(row, lane):
        inside = jnp.logical_and(row >= 96, row < 160)
        return jnp.logical_and(inside, lane == ((row & 31) >> 1))

    return placed((256, 128), match, 0.125)


def feature_spread():
    def match(row, lane):
        inside = jnp.logical_and(lane >= 32, lane < 224)
        return jnp.logical_and(inside, row == ((lane - 32) >> 6) * 16 + ((lane & 31) >> 1))

    return placed((128, 256), match, 0.125)


def brick_join():
    def match(row, lane):
        return row == lane + jnp.where(lane < 64, 0, jnp.where(lane < 192, 64, 128))

    return placed((384, 256), match)


def dot_two(a, b):
    high = a.astype(BF16)
    low = (a - high.astype(F32)).astype(BF16)
    out = dot(jnp.concatenate([high, low], axis=0), b)
    return out[: a.shape[0]] + out[a.shape[0] :]


def leaky(values):
    return jnp.where(values > 0, values, SLOPE * values)


def lanes(count):
    return lax.broadcasted_iota(jnp.int32, (1, count), 1)


def turned_field(volume_in, grads_in, field, volume, feature_grad, held, done):
    pairs = ((volume_in, volume), (grads_in, feature_grad))
    copies = [pltpu.make_async_copy(a, b, done.at[i]) for i, (a, b) in enumerate(pairs)]
    for copy in copies:
        copy.start()
    held[...] = jnp.zeros(held.shape, F32)
    turn = turned()
    copies[1].wait()
    grads = feature_grad[...].astype(F32)
    for s in range(16):
        for i in range(3):
            h = s + i - 1
            if 0 <= h < 16:
                held[4 * s : 4 * s + 4, 16 * i : 16 * i + 16] = grads[:, h, :]
    for t in range(2):
        field[8 + t] = held[32 * t : 32 * t + 32].astype(BF16)
    copies[0].wait()
    for d in range(8):
        stack = jnp.concatenate([volume[c, d].astype(F32) for c in range(4)], axis=0)
        field[d] = dot(turn, stack.astype(BF16)).astype(BF16)


def tall_field(w_third, far_prev, prev, own, nxt, far_nxt, tall, sent, held):
    for d in range(7):
        tall[d] = far_prev[d + 1]
        tall[31 + d] = far_nxt[d]
    for d in range(8):
        tall[7 + d] = prev[d]
        tall[15 + d] = own[d]
        tall[23 + d] = nxt[d]
    held[...] = jnp.zeros(held.shape, F32)
    for k in range(27):
        g, i = divmod(k, 4)
        held[0, 4 * g : 4 * g + 4, 32 * i : 32 * i + 32] = w_third[k].astype(F32)
    for s in range(1, 16):
        held[s, 0:28] = held[0, 0:28]
    for j, part in enumerate((prev, own, nxt)):
        for t in range(2):
            grads = part[8 + t].astype(F32)
            for s in range(8):
                held[8 * t + s, 28 + 4 * j : 32 + 4 * j] = grads[4 * s : 4 * s + 4]
    sent[...] = held[...].astype(BF16)


def forward(
    n_sx, field, w_first, w_second, taps,
    second, mask_a, patch_a, mask_b, patch_b, cells, rows_b, cols,
):
    ix, iy = lax.axis_index("sx"), lax.axis_index("sy")
    left = lanes(128) < 64
    flat = field[...].reshape(3648, 128)
    pairs = column_pairs()
    for half in range(2):
        wide = dot(flat, pairs[:, 256 * half : 256 * half + 256])
        for t in range(2):
            for d in range(38):
                part = wide[96 * d : 96 * d + 96, 128 * t : 128 * t + 128]
                cells[2 * half + t, d] = jnp.where(left, part[0:80], part[8:88]).astype(BF16)
    turned_w = dot_t(unit(16, BF16), w_first[...]).astype(BF16)
    w_a = jnp.concatenate(
        [dot_t(turned_w, taps[256 * p : 256 * p + 256]).astype(BF16) for p in range(8)], axis=0
    )
    w_b = dot_t(unit(32, BF16), w_second[...]).astype(BF16)
    pair = lanes(128) // 64
    for two in range(9):
        rows = []
        for kd in range(4):
            for t in range(4):
                pieces = []
                for d in (2 * two, 2 * two + 1):
                    for a in range(5):
                        pieces.append(cells[t, 2 * d + kd, 16 * a : 16 * a + 16])
                rows.append(jnp.concatenate(pieces, axis=1))
        patch = jnp.concatenate(rows, axis=0)
        pre = dot(w_a, patch)
        act = leaky(pre)
        pool = act[0:16]
        for p in range(1, 8):
            pool = pool + act[16 * p : 16 * p + 16]
        pool = 0.125 * pool
        for t in range(2):
            d = 2 * two + t
            start = 640 * t
            if 7 <= d < 11:
                own = pre[:, start + 128 : start + 512]
                mask_a[d - 7] = jnp.where(own > 0, 1.0, 0.0).astype(BF16)
                patch_a[d - 7] = patch[:, start + 128 : start + 512]
            deep = 4 * ix - 7 + d
            in_depth = jnp.logical_and(deep >= 0, deep < 4 * n_sx)
            kept = []
            for a in range(5):
                row = 4 * iy - 3 + 2 * a + pair
                keep = jnp.logical_and(jnp.logical_and(row >= 0, row < 64), in_depth)
                kept.append(jnp.where(keep, pool[:, start + 128 * a : start + 128 * a + 128], 0.0))
            kept = jnp.concatenate(kept, axis=0)
            swapped = pltpu.roll(kept, 64, 1)
            odd = jnp.where(left, swapped[0:64], swapped[16:80])
            rows_b[d] = jnp.concatenate([kept, odd], axis=0).astype(BF16)
    wide = dot(rows_b[...].reshape(2592, 128), column_shift(64)).astype(BF16)
    for d in range(18):
        for kh in range(3):
            first = 144 * d + 16 * (0, 5, 1)[kh]
            for kw in range(3):
                block = jnp.concatenate(
                    [
                        wide[first + 16 * j : first + 16 * j + 16, 128 * kw : 128 * kw + 128]
                        for j in range(4)
                    ],
                    axis=1,
                )
                cols[d, 16 * (3 * kh + kw) : 16 * (3 * kh + kw) + 16] = block
    for d in range(6):
        patch_b[d] = cols[d + 6]
    row = 2 * iy - 1 + lanes(128) // 32
    in_rows = jnp.logical_and(row >= 0, row < 32)
    acts = []
    for e in range(8):
        act = jnp.zeros((32, 512), F32)
        for d in (2 * e, 2 * e + 1):
            pre = dot(w_b, cols[d : d + 3].reshape(432, 512))
            if 4 <= d < 12:
                mask_b[d - 4] = jnp.where(pre > 0, 1.0, 0.0).astype(BF16)
            act = act + leaky(pre)
        acts.append(act)
    pool = dot_two(jnp.concatenate(acts, axis=0), second_pool())
    for e in range(8):
        deep = 2 * ix - 3 + e
        in_depth = jnp.logical_and(deep >= 0, deep < 2 * n_sx)
        out = pool[32 * e : 32 * e + 32]
        second[e] = jnp.where(jnp.logical_and(in_rows, in_depth), out, 0.0).astype(BF16)


def backward(
    n_sx, prev, own, nxt, got, mask_a, patch_a, mask_b, patch_b, w_second, taps,
    shift_c, shift_d, spread_b,
    parts, w_third, grads, cols_c, grads_c, cols_g, flip_c, flip_b, grads_b, cols_h, held,
):
    ix, iy = lax.axis_index("sx"), lax.axis_index("sy")
    arrived = got[...].astype(F32)
    for s in range(16):
        for g in range(7):
            w_third[4 * s : 4 * s + 4, 128 * g : 128 * g + 128] = arrived[s, 4 * g : 4 * g + 4]
        for j in range(3):
            grads[j, 4 * s : 4 * s + 4] = arrived[s, 28 + 4 * j : 32 + 4 * j]
    wide_w = w_third[...].astype(BF16)
    w_c = wide_w[:, 0:864]
    tall = jnp.concatenate([prev[...], own[...], nxt[...]], axis=2).reshape(256, 384)
    joined = dot(tall, brick_join()).astype(BF16)
    for k in range(9):
        shifted = dot(joined, shift_c[:, 256 * k : 256 * k + 256]).astype(BF16)
        for d in range(8):
            cols_c[d, 32 * k : 32 * k + 32] = shifted[32 * d : 32 * d + 32]
    row = lanes(256) // 32
    mine = jnp.logical_and(row >= 3, row < 5)
    spread_c = feature_spread()
    spreads = [dot(grads[j].astype(BF16), spread_c) for j in range(3)]
    pooled = jnp.zeros((64, 256), F32)
    third_wg = jnp.zeros((64, 864), F32)
    for e in range(1, 7):
        window = cols_c[e - 1 : e + 2].reshape(864, 256)
        pre = dot(w_c, window)
        back = (jnp.where(pre > 0, 1.0, SLOPE) * spreads[(e - 1) // 2]).astype(BF16)
        grads_c[e - 1] = back
        if e in (3, 4):
            pooled = pooled + leaky(pre)
            third_wg = third_wg + dot_t(jnp.where(mine, back, jnp.zeros((), BF16)), window)
    features = dot_two(pooled, third_pool())
    for k in range(9):
        shifted = dot(grads_c[...].reshape(384, 256), shift_c[:, 256 * k : 256 * k + 256])
        shifted = shifted.astype(BF16)
        for e in range(6):
            cols_g[e, 64 * k : 64 * k + 64] = shifted[64 * e : 64 * e + 64]
    for j in range(27):
        k = 26 - j
        flip_c[64 * j : 64 * j + 64, :] = w_third[:, 32 * k : 32 * k + 32]
    back_c = dot_t(unit(32, BF16), flip_c[...].astype(BF16)).astype(BF16)
    ups = [dot(back_c, cols_g[e : e + 3].reshape(1728, 256)) for e in range(4)]
    fine = dot_two(jnp.concatenate(ups, axis=0), spread_b[...])
    row = 4 * iy - 2 + lanes(512) // 64
    in_rows = jnp.logical_and(row >= 0, row < 64)
    row = lanes(512) // 64
    mine = jnp.logical_and(row >= 2, row < 6)
    second_wg = jnp.zeros((32, 432), F32)
    for d in range(1, 7):
        slope = jnp.where(mask_b[d].astype(F32) > 0.5, 1.0, SLOPE)
        deep = 4 * ix - 2 + d
        keep = jnp.logical_and(in_rows, jnp.logical_and(deep >= 0, deep < 4 * n_sx))
        back = jnp.where(keep, slope * fine[32 * (d // 2) : 32 * (d // 2) + 32], 0.0)
        if 2 <= d < 6:
            own_part = jnp.where(mine, back, 0.0).astype(BF16)
            second_wg = second_wg + dot_t(own_part, patch_b[d - 2 : d + 1].reshape(432, 512))
        grads_b[d - 1] = back.astype(BF16)
    for k in range(9):
        shifted = dot(grads_b[...].reshape(192, 512), shift_d[:, 256 * k : 256 * k + 256])
        shifted = shifted.astype(BF16)
        for d in range(6):
            cols_h[d, 32 * k : 32 * k + 32] = shifted[32 * d : 32 * d + 32]
    wb = w_second[...].astype(F32)
    for j in range(27):
        k = 26 - j
        flip_b[:, 32 * j : 32 * j + 32] = wb[16 * k : 16 * k + 16]
    back_b = flip_b[...][:, 0:864].astype(BF16)
    ups = [dot(back_b, cols_h[d : d + 3].reshape(864, 256)) for d in range(4)]
    left = lanes(128) < 64
    blocks = jnp.zeros((128, 256), F32)
    for d in range(4):
        one, two = (pltpu.roll(0.125 * ups[d][:, 128 * t : 128 * t + 128], 64, 1) for t in range(2))
        up = jnp.concatenate(
            [jnp.where(left, 0.0, one), jnp.where(left, one, two), jnp.where(left, two, 0.0)], axis=1
        )
        slope = jnp.where(mask_a[d].astype(F32) > 0.5, 1.0, SLOPE)
        back = (slope * jnp.concatenate([up] * 8, axis=0)).astype(BF16)
        blocks = blocks + dot_t(back, patch_a[d])
    first_wg = jnp.zeros((16, 128), F32)
    for p in range(8):
        first_wg = first_wg + dot_two(
            blocks[16 * p : 16 * p + 16], taps[256 * p : 256 * p + 256]
        )
    third_wg = jnp.concatenate([third_wg, jnp.zeros((64, 32), F32)], axis=1)
    second_wg = jnp.concatenate([second_wg, jnp.zeros((32, 80), F32)], axis=1)
    held[...] = jnp.zeros(held.shape, F32)
    for q in range(32):
        hi, s = divmod(q, 16)
        for g in range(7):
            o = 4 * s + 2 * hi
            held[q, 2 * g : 2 * g + 2] = third_wg[o : o + 2, 128 * g : 128 * g + 128]
        for g in range(4):
            held[q, 14 + g : 15 + g] = second_wg[q : q + 1, 128 * g : 128 * g + 128]
        if hi == 0:
            held[q, 18:19] = first_wg[s : s + 1]
        held[q, 19:23] = features[4 * s : 4 * s + 4]
    parts[...] = held[...].astype(BF16)


def summed(got):
    total = got[0].astype(F32)
    for s in range(1, got.shape[0]):
        total = total + got[s].astype(F32)
    return total


def spread_sum(got, total):
    out = summed(got).astype(BF16)
    for s in range(total.shape[0]):
        total[s] = out


def plane_sum(got, total, features, held):
    spread_sum(got, total)
    hi = lax.rem(lax.axis_index("sx"), 2)
    arrived = got[pl.ds(16 * hi, 16)].astype(F32)
    for o in range(4):
        for s in range(16):
            held[o, s : s + 1] = arrived[s, 19 + o : 20 + o, 0:16]
    features[...] = held[...].astype(BF16)


def last(scale_a, scale_b, scale_c, got, first, second, third, held_a, held_b):
    held_a[...] = jnp.zeros(held_a.shape, F32)
    held_b[...] = jnp.zeros(held_b.shape, F32)
    for q in range(32):
        part = got[q].astype(F32)
        if q < 16:
            held_a[q : q + 1] = part[18:19]
        for g in range(4):
            held_b[q : q + 1, 128 * g : 128 * g + 128] = part[14 + g : 15 + g]
    for hi in range(2):
        part = scale_c * got[16 * hi + lax.axis_index("sy")].astype(F32)
        for k in range(27):
            g, i = divmod(k, 4)
            third[k, 2 * hi : 2 * hi + 2] = part[2 * g : 2 * g + 2, 32 * i : 32 * i + 32]
    turned_a = scale_a * jnp.transpose(held_a[...])
    for k in range(27):
        first[k] = turned_a[4 * k : 4 * k + 4, 0:16]
    for g in range(4):
        turned_b = scale_b * jnp.transpose(held_b[:, 128 * g : 128 * g + 128])
        for j in range(8):
            k = 8 * g + j
            if k < 27:
                second[k] = turned_b[16 * j : 16 * j + 16, 0:32]


def call(body, outs, scratch, *args, space=pltpu.VMEM, copies=0, limit=48 * 1024 * 1024, cost=1e8):
    semaphores = [pltpu.SemaphoreType.DMA((copies,))] if copies else []
    return pl.pallas_call(
        body,
        out_shape=[jax.ShapeDtypeStruct(shape, dtype) for shape, dtype in outs],
        in_specs=[pl.BlockSpec(memory_space=space)] * len(args),
        out_specs=[pl.BlockSpec(memory_space=pltpu.VMEM)] * len(outs),
        scratch_shapes=[pltpu.VMEM(shape, dtype) for shape, dtype in scratch] + semaphores,
        compiler_params=pltpu.CompilerParams(vmem_limit_bytes=limit),
        cost_estimate=pl.CostEstimate(flops=int(cost), bytes_accessed=10**5, transcendentals=0),
    )(*args)


def exchanged(to_prev, to_next, axis, step=1):
    ends = lax.axis_size(axis) - step
    from_prev = lax.ppermute(to_next, axis, [(i, i + step) for i in range(ends)])
    from_next = lax.ppermute(to_prev, axis, [(i + step, i) for i in range(ends)])
    return from_prev, from_next


def table(values, dtype=BF16):
    return jnp.asarray(values, dtype)


def shards(volume, w_first, w_second, w_third, feature_grad):
    n_sx, n_sy = lax.axis_size("sx"), lax.axis_size("sy")
    n_z = n_sx // 2
    cells = volume.shape[1] * volume.shape[2] * volume.shape[3] * n_sx * n_sy
    first_w = jnp.pad(w_first.transpose(2, 3, 4, 1, 0).reshape(108, 16), ((0, 20), (0, 0)))
    second_w = w_second.transpose(2, 3, 4, 1, 0).reshape(432, 32)
    third_w = w_third.transpose(2, 3, 4, 0, 1).reshape(27, 4, 32)
    taps = table(block_taps())

    (field,) = call(
        turned_field,
        [((10, 32, 128), BF16)],
        [((4, 8, 8, 128), BF16), ((4, 16, 16), BF16), ((64, 128), F32)],
        volume, feature_grad.reshape(4, 16, 16),
        space=pl.ANY, copies=2, limit=None,
    )
    prev, nxt = exchanged(field, field, "sx")
    far_prev, far_nxt = exchanged(field[:8], field[:8], "sx", 2)
    tall, sent = call(
        tall_field,
        [((38, 32, 128), BF16), ((16, 40, 128), BF16)],
        [((16, 40, 128), F32)],
        third_w, far_prev, prev, field, nxt, far_nxt,
    )
    got = lax.all_to_all(sent, "sy", 0, 0, tiled=True)
    prev, nxt = exchanged(tall, tall, "sy")
    field = jnp.concatenate([prev[:, 4:], tall, nxt, nxt[:, :4]], axis=1)
    second, mask_a, patch_a, mask_b, patch_b = call(
        lambda *refs: forward(n_sx, *refs),
        [
            ((8, 32, 128), BF16), ((4, 128, 384), BF16), ((4, 256, 384), BF16),
            ((8, 32, 512), BF16), ((6, 144, 512), BF16),
        ],
        [((4, 38, 80, 128), BF16), ((18, 144, 128), BF16), ((18, 144, 512), BF16)],
        field, first_w, second_w, taps, cost=5e9,
    )
    prev, nxt = exchanged(second, second, "sy")
    (parts,) = call(
        lambda *refs: backward(n_sx, *refs),
        [((32, 24, 128), BF16)],
        [
            ((64, 896), F32), ((3, 64, 128), F32), ((8, 288, 256), BF16), ((6, 64, 256), BF16),
            ((6, 576, 256), BF16), ((1728, 32), F32), ((16, 896), F32),
            ((6, 32, 512), BF16), ((6, 288, 256), BF16), ((32, 24, 128), F32),
        ],
        prev, second, nxt, got, mask_a, patch_a, mask_b, patch_b, second_w, taps,
        table(tap_shift(8, 32, 0, 8)), table(tap_shift(8, 64, 2, 4)),
        table(second_spread()), cost=11e9,
    )
    planes = [[32 * z + i for i in range(32)] for z in range(n_z)]
    lines = [[2 * z + hi for z in range(n_z)] for hi in range(2)]
    both = ("sx", "sy")
    got = lax.all_to_all(parts, both, 0, 0, tiled=True, axis_index_groups=planes)
    total, features = call(
        plane_sum, [((n_z, 24, 128), BF16), ((4, 16, 16), BF16)], [((4, 16, 16), F32)], got
    )
    got = lax.all_to_all(total, "sx", 0, 0, tiled=True, axis_index_groups=lines)
    (total,) = call(spread_sum, [((32, 24, 128), BF16)], [], got)
    got = lax.all_to_all(total, both, 0, 0, tiled=True, axis_index_groups=planes)
    scales = (64.0 / math.sqrt(cells), 8.0 / math.sqrt(cells / 8), 1.0 / math.sqrt(cells / 64))
    first, second, third = call(
        lambda *refs: last(*scales, *refs),
        [((27, 4, 16), F32), ((27, 16, 32), F32), ((27, 4, 32), F32)],
        [((128, 128), F32), ((128, 512), F32)],
        got,
    )
    first_grad = first.reshape(3, 3, 3, 4, 16).transpose(4, 3, 0, 1, 2)
    second_grad = second.reshape(3, 3, 3, 16, 32).transpose(4, 3, 0, 1, 2)
    third_grad = third.reshape(3, 3, 3, 4, 32).transpose(3, 4, 0, 1, 2)
    return (features.reshape(4, 1, 16, 16), first_grad, second_grad, third_grad)


def solution(mesh):
    in_specs = (
        P(None, "sx", "sy", None),
        P(),
        P(),
        P("sy", None, None, None, None),
        P("sy", "sx", None, None),
    )
    out_specs = (P("sy", "sx", None, None), P(), P(), P("sy", None, None, None, None))
    return jax.shard_map(shards, mesh=mesh, in_specs=in_specs, out_specs=out_specs, check_vma=False)
```

```python
import math

import jax
import jax.numpy as jnp
import numpy as np
from jax import lax
from jax.experimental import pallas as pl
from jax.experimental.pallas import tpu as pltpu
from jax.sharding import PartitionSpec as P

SLOPE = 0.3
BF16 = jnp.bfloat16
F32 = jnp.float32


def tap_shift(rows, cols, out_first, out_rows):
    table = np.zeros((rows, cols, 3, 3, out_rows, cols), np.float32)
    for kh in range(3):
        for kw in range(3):
            for r in range(out_rows):
                for w in range(cols):
                    row, col = out_first + r + kh - 1, w + kw - 1
                    if 0 <= row < rows and 0 <= col < cols:
                        table[row, col, kh, kw, r, w] = 1
    return table.reshape(rows * cols, 9 * out_rows * cols)


def second_spread():
    table = np.zeros((8, 32, 8, 64), np.float32)
    for r in range(8):
        for w in range(64):
            table[2 + r // 2, w // 2, r, w] = 0.125
    return table.reshape(256, 512)


def block_taps():
    table = np.zeros((2, 2, 2, 4, 4, 4, 4, 128), np.float32)
    for pd, ph, pw in np.ndindex(2, 2, 2):
        for kd, kh, kw, c in np.ndindex(3, 3, 3, 4):
            at = ((kd * 3 + kh) * 3 + kw) * 4 + c
            table[pd, ph, pw, kd + pd, kw + pw, kh + ph, c, at] = 1
    return table.reshape(2048, 128)


def dot(a, b):
    return lax.dot_general(a, b, (((1,), (0,)), ((), ())), preferred_element_type=F32)


def dot_t(a, b):
    return lax.dot_general(a, b, (((1,), (1,)), ((), ())), preferred_element_type=F32)


def placed(shape, match, value=1.0, dtype=BF16):
    row, lane = (lax.broadcasted_iota(jnp.int32, shape, axis) for axis in range(2))
    return jnp.where(match(row, lane), value, 0.0).astype(dtype)


def unit(size, dtype):
    return placed((size, size), lambda row, lane: row == lane, 1.0, dtype)


def turned():
    return placed((32, 32), lambda row, lane: lane == (row & 3) * 8 + (row >> 2))


def column_shift(cols):
    def match(row, lane):
        to = (lane & 127) + (lane >> 7) - 1
        return jnp.logical_and(row == to, (row // cols) == (lane & 127) // cols)

    return placed((128, 384), match)


def column_pairs():
    return placed((128, 512), lambda row, lane: row == 2 * (lane & 63) + (lane >> 7) - 1)


def second_pool():
    return placed((512, 128), lambda row, lane: lane == (row >> 7) * 32 + ((row & 63) >> 1), 0.125)


def third_pool():
    def match(row, lane):
        inside = jnp.logical_and(row >= 96, row < 160)
        return jnp.logical_and(inside, lane == ((row & 31) >> 1))

    return placed((256, 128), match, 0.125)


def feature_spread():
    def match(row, lane):
        inside = jnp.logical_and(lane >= 32, lane < 224)
        return jnp.logical_and(inside, row == ((lane - 32) >> 6) * 16 + ((lane & 31) >> 1))

    return placed((128, 256), match, 0.125)


def brick_join():
    def match(row, lane):
        return row == lane + jnp.where(lane < 64, 0, jnp.where(lane < 192, 64, 128))

    return placed((384, 256), match)


def dot_two(a, b):
    high = a.astype(BF16)
    low = (a - high.astype(F32)).astype(BF16)
    out = dot(jnp.concatenate([high, low], axis=0), b)
    return out[: a.shape[0]] + out[a.shape[0] :]


def leaky(values):
    return jnp.where(values > 0, values, SLOPE * values)


def lanes(count):
    return lax.broadcasted_iota(jnp.int32, (1, count), 1)


def turned_field(volume_in, grads_in, weights_in, field, volume, feature_grad, w_third, held, done):
    pairs = ((volume_in, volume), (grads_in, feature_grad), (weights_in, w_third))
    copies = [pltpu.make_async_copy(a, b, done.at[i]) for i, (a, b) in enumerate(pairs)]
    for copy in copies:
        copy.start()
    held[...] = jnp.zeros(held.shape, F32)
    turn = turned()
    copies[1].wait()
    grads = feature_grad[...].astype(F32)
    for s in range(16):
        for i in range(3):
            h = s + i - 1
            if 0 <= h < 16:
                held[4 * s : 4 * s + 4, 16 * i : 16 * i + 16] = grads[:, h, :]
    copies[2].wait()
    for k in range(27):
        g, i = divmod(k, 4)
        held[64 + 4 * g : 68 + 4 * g, 32 * i : 32 * i + 32] = w_third[k].astype(F32)
    for t in range(3):
        field[8 + t] = held[32 * t : 32 * t + 32].astype(BF16)
    copies[0].wait()
    for d in range(8):
        stack = jnp.concatenate([volume[c, d].astype(F32) for c in range(4)], axis=0)
        field[d] = dot(turn, stack.astype(BF16)).astype(BF16)


def tall_field(far_prev, prev, own, nxt, far_nxt, tall, sent, held):
    for d in range(7):
        tall[d] = far_prev[d + 1]
        tall[31 + d] = far_nxt[d]
    for d in range(8):
        tall[7 + d] = prev[d]
        tall[15 + d] = own[d]
        tall[23 + d] = nxt[d]
    weights = own[10].astype(F32)[0:28]
    for s in range(16):
        held[s, 0:28] = weights
    for j, part in enumerate((prev, own, nxt)):
        for t in range(2):
            grads = part[8 + t].astype(F32)
            for s in range(8):
                held[8 * t + s, 28 + 4 * j : 32 + 4 * j] = grads[4 * s : 4 * s + 4]
    sent[...] = held[...].astype(BF16)


def forward(
    n_sx, field, w_first, w_second, taps,
    second, mask_a, patch_a, mask_b, patch_b, cells, rows_b, cols,
):
    ix, iy = lax.axis_index("sx"), lax.axis_index("sy")
    left = lanes(128) < 64
    flat = field[...].reshape(3648, 128)
    pairs = column_pairs()
    for half in range(2):
        wide = dot(flat, pairs[:, 256 * half : 256 * half + 256])
        for t in range(2):
            for d in range(38):
                part = wide[96 * d : 96 * d + 96, 128 * t : 128 * t + 128]
                cells[2 * half + t, d] = jnp.where(left, part[0:80], part[8:88]).astype(BF16)
    turned_w = dot_t(unit(16, BF16), w_first[...]).astype(BF16)
    w_a = jnp.concatenate(
        [dot_t(turned_w, taps[256 * p : 256 * p + 256]).astype(BF16) for p in range(8)], axis=0
    )
    w_b = dot_t(unit(32, BF16), w_second[...]).astype(BF16)
    pair = lanes(128) // 64
    for two in range(9):
        rows = []
        for kd in range(4):
            for t in range(4):
                pieces = []
                for d in (2 * two, 2 * two + 1):
                    for a in range(5):
                        pieces.append(cells[t, 2 * d + kd, 16 * a : 16 * a + 16])
                rows.append(jnp.concatenate(pieces, axis=1))
        patch = jnp.concatenate(rows, axis=0)
        pre = dot(w_a, patch)
        act = leaky(pre)
        pool = act[0:16]
        for p in range(1, 8):
            pool = pool + act[16 * p : 16 * p + 16]
        pool = 0.125 * pool
        for t in range(2):
            d = 2 * two + t
            start = 640 * t
            if 7 <= d < 11:
                own = pre[:, start + 128 : start + 512]
                mask_a[d - 7] = jnp.where(own > 0, 1.0, 0.0).astype(BF16)
                patch_a[d - 7] = patch[:, start + 128 : start + 512]
            deep = 4 * ix - 7 + d
            in_depth = jnp.logical_and(deep >= 0, deep < 4 * n_sx)
            kept = []
            for a in range(5):
                row = 4 * iy - 3 + 2 * a + pair
                keep = jnp.logical_and(jnp.logical_and(row >= 0, row < 64), in_depth)
                kept.append(jnp.where(keep, pool[:, start + 128 * a : start + 128 * a + 128], 0.0))
            kept = jnp.concatenate(kept, axis=0)
            swapped = pltpu.roll(kept, 64, 1)
            odd = jnp.where(left, swapped[0:64], swapped[16:80])
            rows_b[d] = jnp.concatenate([kept, odd], axis=0).astype(BF16)
    wide = dot(rows_b[...].reshape(2592, 128), column_shift(64)).astype(BF16)
    for d in range(18):
        for kh in range(3):
            first = 144 * d + 16 * (0, 5, 1)[kh]
            for kw in range(3):
                block = jnp.concatenate(
                    [
                        wide[first + 16 * j : first + 16 * j + 16, 128 * kw : 128 * kw + 128]
                        for j in range(4)
                    ],
                    axis=1,
                )
                cols[d, 16 * (3 * kh + kw) : 16 * (3 * kh + kw) + 16] = block
    for d in range(6):
        patch_b[d] = cols[d + 6]
    row = 2 * iy - 1 + lanes(128) // 32
    in_rows = jnp.logical_and(row >= 0, row < 32)
    acts = []
    for e in range(8):
        act = jnp.zeros((32, 512), F32)
        for d in (2 * e, 2 * e + 1):
            pre = dot(w_b, cols[d : d + 3].reshape(432, 512))
            if 4 <= d < 12:
                mask_b[d - 4] = jnp.where(pre > 0, 1.0, 0.0).astype(BF16)
            act = act + leaky(pre)
        acts.append(act)
    pool = dot_two(jnp.concatenate(acts, axis=0), second_pool())
    for e in range(8):
        deep = 2 * ix - 3 + e
        in_depth = jnp.logical_and(deep >= 0, deep < 2 * n_sx)
        out = pool[32 * e : 32 * e + 32]
        second[e] = jnp.where(jnp.logical_and(in_rows, in_depth), out, 0.0).astype(BF16)


def backward(
    n_sx, prev, own, nxt, got, mask_a, patch_a, mask_b, patch_b, w_second, taps,
    shift_c, shift_d, spread_b,
    parts, w_third, grads, cols_c, grads_c, cols_g, flip_c, flip_b, grads_b, cols_h, held,
):
    ix, iy = lax.axis_index("sx"), lax.axis_index("sy")
    arrived = got[...].astype(F32)
    for s in range(16):
        for g in range(7):
            w_third[4 * s : 4 * s + 4, 128 * g : 128 * g + 128] = arrived[s, 4 * g : 4 * g + 4]
        for j in range(3):
            grads[j, 4 * s : 4 * s + 4] = arrived[s, 28 + 4 * j : 32 + 4 * j]
    wide_w = w_third[...].astype(BF16)
    w_c = wide_w[:, 0:864]
    tall = jnp.concatenate([prev[...], own[...], nxt[...]], axis=2).reshape(256, 384)
    joined = dot(tall, brick_join()).astype(BF16)
    for k in range(9):
        shifted = dot(joined, shift_c[:, 256 * k : 256 * k + 256]).astype(BF16)
        for d in range(8):
            cols_c[d, 32 * k : 32 * k + 32] = shifted[32 * d : 32 * d + 32]
    row = lanes(256) // 32
    mine = jnp.logical_and(row >= 3, row < 5)
    spread_c = feature_spread()
    spreads = [dot(grads[j].astype(BF16), spread_c) for j in range(3)]
    pooled = jnp.zeros((64, 256), F32)
    third_wg = jnp.zeros((64, 864), F32)
    for e in range(1, 7):
        window = cols_c[e - 1 : e + 2].reshape(864, 256)
        pre = dot(w_c, window)
        back = (jnp.where(pre > 0, 1.0, SLOPE) * spreads[(e - 1) // 2]).astype(BF16)
        grads_c[e - 1] = back
        if e in (3, 4):
            pooled = pooled + leaky(pre)
            third_wg = third_wg + dot_t(jnp.where(mine, back, jnp.zeros((), BF16)), window)
    features = dot_two(pooled, third_pool())
    for k in range(9):
        shifted = dot(grads_c[...].reshape(384, 256), shift_c[:, 256 * k : 256 * k + 256])
        shifted = shifted.astype(BF16)
        for e in range(6):
            cols_g[e, 64 * k : 64 * k + 64] = shifted[64 * e : 64 * e + 64]
    for j in range(27):
        k = 26 - j
        flip_c[64 * j : 64 * j + 64, :] = w_third[:, 32 * k : 32 * k + 32]
    back_c = dot_t(unit(32, BF16), flip_c[...].astype(BF16)).astype(BF16)
    ups = [dot(back_c, cols_g[e : e + 3].reshape(1728, 256)) for e in range(4)]
    fine = dot_two(jnp.concatenate(ups, axis=0), spread_b[...])
    row = 4 * iy - 2 + lanes(512) // 64
    in_rows = jnp.logical_and(row >= 0, row < 64)
    row = lanes(512) // 64
    mine = jnp.logical_and(row >= 2, row < 6)
    second_wg = jnp.zeros((32, 432), F32)
    for d in range(1, 7):
        slope = jnp.where(mask_b[d].astype(F32) > 0.5, 1.0, SLOPE)
        deep = 4 * ix - 2 + d
        keep = jnp.logical_and(in_rows, jnp.logical_and(deep >= 0, deep < 4 * n_sx))
        back = jnp.where(keep, slope * fine[32 * (d // 2) : 32 * (d // 2) + 32], 0.0)
        if 2 <= d < 6:
            own_part = jnp.where(mine, back, 0.0).astype(BF16)
            second_wg = second_wg + dot_t(own_part, patch_b[d - 2 : d + 1].reshape(432, 512))
        grads_b[d - 1] = back.astype(BF16)
    for k in range(9):
        shifted = dot(grads_b[...].reshape(192, 512), shift_d[:, 256 * k : 256 * k + 256])
        shifted = shifted.astype(BF16)
        for d in range(6):
            cols_h[d, 32 * k : 32 * k + 32] = shifted[32 * d : 32 * d + 32]
    wb = w_second[...].astype(F32)
    for j in range(27):
        k = 26 - j
        flip_b[:, 32 * j : 32 * j + 32] = wb[16 * k : 16 * k + 16]
    back_b = flip_b[...][:, 0:864].astype(BF16)
    ups = [dot(back_b, cols_h[d : d + 3].reshape(864, 256)) for d in range(4)]
    left = lanes(128) < 64
    blocks = jnp.zeros((128, 256), F32)
    for d in range(4):
        one, two = (pltpu.roll(0.125 * ups[d][:, 128 * t : 128 * t + 128], 64, 1) for t in range(2))
        up = jnp.concatenate(
            [jnp.where(left, 0.0, one), jnp.where(left, one, two), jnp.where(left, two, 0.0)], axis=1
        )
        slope = jnp.where(mask_a[d].astype(F32) > 0.5, 1.0, SLOPE)
        back = (slope * jnp.concatenate([up] * 8, axis=0)).astype(BF16)
        blocks = blocks + dot_t(back, patch_a[d])
    first_wg = jnp.zeros((16, 128), F32)
    for p in range(8):
        first_wg = first_wg + dot_two(
            blocks[16 * p : 16 * p + 16], taps[256 * p : 256 * p + 256]
        )
    third_wg = jnp.concatenate([third_wg, jnp.zeros((64, 32), F32)], axis=1)
    second_wg = jnp.concatenate([second_wg, jnp.zeros((32, 80), F32)], axis=1)
    held[...] = jnp.zeros(held.shape, F32)
    for q in range(32):
        hi, s = divmod(q, 16)
        for g in range(7):
            o = 4 * s + 2 * hi
            held[q, 2 * g : 2 * g + 2] = third_wg[o : o + 2, 128 * g : 128 * g + 128]
        for g in range(4):
            held[q, 14 + g : 15 + g] = second_wg[q : q + 1, 128 * g : 128 * g + 128]
        if hi == 0:
            held[q, 18:19] = first_wg[s : s + 1]
        held[q, 19:23] = features[4 * s : 4 * s + 4]
    parts[...] = held[...].astype(BF16)


def summed(got):
    total = got[0].astype(F32)
    for s in range(1, got.shape[0]):
        total = total + got[s].astype(F32)
    return total


def spread_sum(got, total):
    out = summed(got).astype(BF16)
    for s in range(total.shape[0]):
        total[s] = out


def plane_sum(got, total, features, held):
    spread_sum(got, total)
    hi = lax.rem(lax.axis_index("sx"), 2)
    arrived = got[pl.ds(16 * hi, 16)].astype(F32)
    for o in range(4):
        for s in range(16):
            held[o, s : s + 1] = arrived[s, 19 + o : 20 + o, 0:16]
    features[...] = held[...].astype(BF16)


def last(scale_a, scale_b, scale_c, got, first, second, third, held_a, held_b):
    held_a[...] = jnp.zeros(held_a.shape, F32)
    held_b[...] = jnp.zeros(held_b.shape, F32)
    for q in range(32):
        part = got[q].astype(F32)
        if q < 16:
            held_a[q : q + 1] = part[18:19]
        for g in range(4):
            held_b[q : q + 1, 128 * g : 128 * g + 128] = part[14 + g : 15 + g]
    for hi in range(2):
        part = scale_c * got[16 * hi + lax.axis_index("sy")].astype(F32)
        for k in range(27):
            g, i = divmod(k, 4)
            third[k, 2 * hi : 2 * hi + 2] = part[2 * g : 2 * g + 2, 32 * i : 32 * i + 32]
    turned_a = scale_a * jnp.transpose(held_a[...])
    for k in range(27):
        first[k] = turned_a[4 * k : 4 * k + 4, 0:16]
    for g in range(4):
        turned_b = scale_b * jnp.transpose(held_b[:, 128 * g : 128 * g + 128])
        for j in range(8):
            k = 8 * g + j
            if k < 27:
                second[k] = turned_b[16 * j : 16 * j + 16, 0:32]


def call(body, outs, scratch, *args, space=pltpu.VMEM, copies=0, limit=48 * 1024 * 1024, cost=1e8):
    semaphores = [pltpu.SemaphoreType.DMA((copies,))] if copies else []
    return pl.pallas_call(
        body,
        out_shape=[jax.ShapeDtypeStruct(shape, dtype) for shape, dtype in outs],
        in_specs=[pl.BlockSpec(memory_space=space)] * len(args),
        out_specs=[pl.BlockSpec(memory_space=pltpu.VMEM)] * len(outs),
        scratch_shapes=[pltpu.VMEM(shape, dtype) for shape, dtype in scratch] + semaphores,
        compiler_params=pltpu.CompilerParams(vmem_limit_bytes=limit),
        cost_estimate=pl.CostEstimate(flops=int(cost), bytes_accessed=10**5, transcendentals=0),
    )(*args)


def exchanged(to_prev, to_next, axis, step=1):
    ends = lax.axis_size(axis) - step
    from_prev = lax.ppermute(to_next, axis, [(i, i + step) for i in range(ends)])
    from_next = lax.ppermute(to_prev, axis, [(i + step, i) for i in range(ends)])
    return from_prev, from_next


def table(values, dtype=BF16):
    return jnp.asarray(values, dtype)


def shards(volume, w_first, w_second, w_third, feature_grad):
    n_sx, n_sy = lax.axis_size("sx"), lax.axis_size("sy")
    n_z = n_sx // 2
    cells = volume.shape[1] * volume.shape[2] * volume.shape[3] * n_sx * n_sy
    first_w = jnp.pad(w_first.transpose(2, 3, 4, 1, 0).reshape(108, 16), ((0, 20), (0, 0)))
    second_w = w_second.transpose(2, 3, 4, 1, 0).reshape(432, 32)
    third_w = w_third.transpose(2, 3, 4, 0, 1).reshape(27, 4, 32)
    taps = table(block_taps())

    (field,) = call(
        turned_field,
        [((11, 32, 128), BF16)],
        [((4, 8, 8, 128), BF16), ((4, 16, 16), BF16), ((27, 4, 32), BF16), ((96, 128), F32)],
        volume, feature_grad.reshape(4, 16, 16), third_w,
        space=pl.ANY, copies=3, limit=None,
    )
    prev, nxt = exchanged(field, field, "sx")
    far_prev, far_nxt = exchanged(field, field, "sx", 2)
    tall, sent = call(
        tall_field,
        [((38, 32, 128), BF16), ((16, 40, 128), BF16)],
        [((16, 40, 128), F32)],
        far_prev, prev, field, nxt, far_nxt,
    )
    got = lax.all_to_all(sent, "sy", 0, 0, tiled=True)
    prev, nxt = exchanged(tall, tall, "sy")
    field = jnp.concatenate([prev[:, 4:], tall, nxt, nxt[:, :4]], axis=1)
    field, got = lax.optimization_barrier((field, got))
    second, mask_a, patch_a, mask_b, patch_b = call(
        lambda *refs: forward(n_sx, *refs),
        [
            ((8, 32, 128), BF16), ((4, 128, 384), BF16), ((4, 256, 384), BF16),
            ((8, 32, 512), BF16), ((6, 144, 512), BF16),
        ],
        [((4, 38, 80, 128), BF16), ((18, 144, 128), BF16), ((18, 144, 512), BF16)],
        field, first_w, second_w, taps, cost=5e9,
    )
    prev, nxt = exchanged(second, second, "sy")
    (parts,) = call(
        lambda *refs: backward(n_sx, *refs),
        [((32, 24, 128), BF16)],
        [
            ((64, 896), F32), ((3, 64, 128), F32), ((8, 288, 256), BF16), ((6, 64, 256), BF16),
            ((6, 576, 256), BF16), ((1728, 32), F32), ((16, 896), F32),
            ((6, 32, 512), BF16), ((6, 288, 256), BF16), ((32, 24, 128), F32),
        ],
        prev, second, nxt, got, mask_a, patch_a, mask_b, patch_b, second_w, taps,
        table(tap_shift(8, 32, 0, 8)), table(tap_shift(8, 64, 2, 4)),
        table(second_spread()), cost=11e9,
    )
    planes = [[32 * z + i for i in range(32)] for z in range(n_z)]
    lines = [[2 * z + hi for z in range(n_z)] for hi in range(2)]
    both = ("sx", "sy")
    got = lax.all_to_all(parts, both, 0, 0, tiled=True, axis_index_groups=planes)
    total, features = call(
        plane_sum, [((n_z, 24, 128), BF16), ((4, 16, 16), BF16)], [((4, 16, 16), F32)], got
    )
    got = lax.all_to_all(total, "sx", 0, 0, tiled=True, axis_index_groups=lines)
    (total,) = call(spread_sum, [((32, 24, 128), BF16)], [], got)
    got = lax.all_to_all(total, both, 0, 0, tiled=True, axis_index_groups=planes)
    scales = (64.0 / math.sqrt(cells), 8.0 / math.sqrt(cells / 8), 1.0 / math.sqrt(cells / 64))
    first, second, third = call(
        lambda *refs: last(*scales, *refs),
        [((27, 4, 16), F32), ((27, 16, 32), F32), ((27, 4, 32), F32)],
        [((128, 128), F32), ((128, 512), F32)],
        got,
    )
    first_grad = first.reshape(3, 3, 3, 4, 16).transpose(4, 3, 0, 1, 2)
    second_grad = second.reshape(3, 3, 3, 16, 32).transpose(4, 3, 0, 1, 2)
    third_grad = third.reshape(3, 3, 3, 4, 32).transpose(3, 4, 0, 1, 2)
    return (features.reshape(4, 1, 16, 16), first_grad, second_grad, third_grad)


def solution(mesh):
    in_specs = (
        P(None, "sx", "sy", None),
        P(),
        P(),
        P("sy", None, None, None, None),
        P("sy", "sx", None, None),
    )
    out_specs = (P("sy", "sx", None, None), P(), P(), P("sy", None, None, None, None))
    return jax.shard_map(shards, mesh=mesh, in_specs=in_specs, out_specs=out_specs, check_vma=False)
```

```python
import math

import jax
import jax.numpy as jnp
import numpy as np
from jax import lax
from jax.experimental import pallas as pl
from jax.experimental.pallas import tpu as pltpu
from jax.sharding import PartitionSpec as P

SLOPE = 0.3
BF16 = jnp.bfloat16
F32 = jnp.float32


def tap_shift(rows, cols, out_first, out_rows):
    table = np.zeros((rows, cols, 3, 3, out_rows, cols), np.float32)
    for kh in range(3):
        for kw in range(3):
            for r in range(out_rows):
                for w in range(cols):
                    row, col = out_first + r + kh - 1, w + kw - 1
                    if 0 <= row < rows and 0 <= col < cols:
                        table[row, col, kh, kw, r, w] = 1
    return table.reshape(rows * cols, 9 * out_rows * cols)


def second_spread():
    table = np.zeros((8, 32, 8, 64), np.float32)
    for r in range(8):
        for w in range(64):
            table[2 + r // 2, w // 2, r, w] = 0.125
    return table.reshape(256, 512)


def block_taps():
    table = np.zeros((2, 2, 2, 4, 4, 4, 4, 128), np.float32)
    for pd, ph, pw in np.ndindex(2, 2, 2):
        for kd, kh, kw, c in np.ndindex(3, 3, 3, 4):
            at = ((kd * 3 + kh) * 3 + kw) * 4 + c
            table[pd, ph, pw, kd + pd, kw + pw, kh + ph, c, at] = 1
    return table.reshape(2048, 128)


def dot(a, b):
    return lax.dot_general(a, b, (((1,), (0,)), ((), ())), preferred_element_type=F32)


def dot_t(a, b):
    return lax.dot_general(a, b, (((1,), (1,)), ((), ())), preferred_element_type=F32)


def placed(shape, match, value=1.0, dtype=BF16):
    row, lane = (lax.broadcasted_iota(jnp.int32, shape, axis) for axis in range(2))
    return jnp.where(match(row, lane), value, 0.0).astype(dtype)


def unit(size, dtype):
    return placed((size, size), lambda row, lane: row == lane, 1.0, dtype)


def turned():
    return placed((32, 32), lambda row, lane: lane == (row & 3) * 8 + (row >> 2))


def column_shift(cols):
    def match(row, lane):
        to = (lane & 127) + (lane >> 7) - 1
        return jnp.logical_and(row == to, (row // cols) == (lane & 127) // cols)

    return placed((128, 384), match)


def column_pairs():
    return placed((128, 512), lambda row, lane: row == 2 * (lane & 63) + (lane >> 7) - 1)


def second_pool():
    return placed((512, 128), lambda row, lane: lane == (row >> 7) * 32 + ((row & 63) >> 1), 0.125)


def third_pool():
    def match(row, lane):
        inside = jnp.logical_and(row >= 96, row < 160)
        return jnp.logical_and(inside, lane == ((row & 31) >> 1))

    return placed((256, 128), match, 0.125)


def feature_spread():
    def match(row, lane):
        inside = jnp.logical_and(lane >= 32, lane < 224)
        return jnp.logical_and(inside, row == ((lane - 32) >> 6) * 16 + ((lane & 31) >> 1))

    return placed((128, 256), match, 0.125)


def brick_join():
    def match(row, lane):
        return row == lane + jnp.where(lane < 64, 0, jnp.where(lane < 192, 64, 128))

    return placed((384, 256), match)


def dot_two(a, b):
    high = a.astype(BF16)
    low = (a - high.astype(F32)).astype(BF16)
    out = dot(jnp.concatenate([high, low], axis=0), b)
    return out[: a.shape[0]] + out[a.shape[0] :]


def leaky(values):
    return jnp.where(values > 0, values, SLOPE * values)


def lanes(count):
    return lax.broadcasted_iota(jnp.int32, (1, count), 1)


def turned_field(volume_in, grads_in, weights_in, field, volume, feature_grad, w_third, held, done):
    pairs = ((volume_in, volume), (grads_in, feature_grad), (weights_in, w_third))
    copies = [pltpu.make_async_copy(a, b, done.at[i]) for i, (a, b) in enumerate(pairs)]
    for copy in copies:
        copy.start()
    held[...] = jnp.zeros(held.shape, F32)
    turn = turned()
    copies[1].wait()
    grads = feature_grad[...].astype(F32)
    for s in range(16):
        for i in range(3):
            h = s + i - 1
            if 0 <= h < 16:
                held[4 * s : 4 * s + 4, 16 * i : 16 * i + 16] = grads[:, h, :]
    copies[2].wait()
    for k in range(27):
        g, i = divmod(k, 4)
        held[64 + 4 * g : 68 + 4 * g, 32 * i : 32 * i + 32] = w_third[k].astype(F32)
    for t in range(3):
        field[8 + t] = held[32 * t : 32 * t + 32].astype(BF16)
    copies[0].wait()
    for d in range(8):
        stack = jnp.concatenate([volume[c, d].astype(F32) for c in range(4)], axis=0)
        field[d] = dot(turn, stack.astype(BF16)).astype(BF16)


def tall_field(far_prev, prev, own, nxt, far_nxt, tall, sent, held):
    for d in range(7):
        tall[d] = far_prev[d + 1]
        tall[31 + d] = far_nxt[d]
    for d in range(8):
        tall[7 + d] = prev[d]
        tall[15 + d] = own[d]
        tall[23 + d] = nxt[d]
    weights = own[10].astype(F32)[0:28]
    for s in range(16):
        held[s, 0:28] = weights
    for j, part in enumerate((prev, own, nxt)):
        for t in range(2):
            grads = part[8 + t].astype(F32)
            for s in range(8):
                held[8 * t + s, 28 + 4 * j : 32 + 4 * j] = grads[4 * s : 4 * s + 4]
    sent[...] = held[...].astype(BF16)


def forward(
    n_sx, field, w_first, w_second, taps,
    second, mask_a, patch_a, mask_b, patch_b, cells, rows_b, cols,
):
    ix, iy = lax.axis_index("sx"), lax.axis_index("sy")
    left = lanes(128) < 64
    flat = field[...].reshape(3648, 128)
    pairs = column_pairs()
    for half in range(2):
        wide = dot(flat, pairs[:, 256 * half : 256 * half + 256])
        for t in range(2):
            for d in range(38):
                part = wide[96 * d : 96 * d + 96, 128 * t : 128 * t + 128]
                cells[2 * half + t, d] = jnp.where(left, part[0:80], part[8:88]).astype(BF16)
    turned_w = dot_t(unit(16, BF16), w_first[...]).astype(BF16)
    w_a = jnp.concatenate(
        [dot_t(turned_w, taps[256 * p : 256 * p + 256]).astype(BF16) for p in range(8)], axis=0
    )
    w_b = dot_t(unit(32, BF16), w_second[...]).astype(BF16)
    pair = lanes(128) // 64
    for two in range(9):
        rows = []
        for kd in range(4):
            for t in range(4):
                pieces = []
                for d in (2 * two, 2 * two + 1):
                    for a in range(5):
                        pieces.append(cells[t, 2 * d + kd, 16 * a : 16 * a + 16])
                rows.append(jnp.concatenate(pieces, axis=1))
        patch = jnp.concatenate(rows, axis=0)
        pre = dot(w_a, patch)
        act = leaky(pre)
        pool = act[0:16]
        for p in range(1, 8):
            pool = pool + act[16 * p : 16 * p + 16]
        pool = 0.125 * pool
        for t in range(2):
            d = 2 * two + t
            start = 640 * t
            if 7 <= d < 11:
                own = pre[:, start + 128 : start + 512]
                mask_a[d - 7] = jnp.where(own > 0, 1.0, 0.0).astype(BF16)
                patch_a[d - 7] = patch[:, start + 128 : start + 512]
            deep = 4 * ix - 7 + d
            in_depth = jnp.logical_and(deep >= 0, deep < 4 * n_sx)
            kept = []
            for a in range(5):
                row = 4 * iy - 3 + 2 * a + pair
                keep = jnp.logical_and(jnp.logical_and(row >= 0, row < 64), in_depth)
                kept.append(jnp.where(keep, pool[:, start + 128 * a : start + 128 * a + 128], 0.0))
            kept = jnp.concatenate(kept, axis=0)
            swapped = pltpu.roll(kept, 64, 1)
            odd = jnp.where(left, swapped[0:64], swapped[16:80])
            rows_b[d] = jnp.concatenate([kept, odd], axis=0).astype(BF16)
    wide = dot(rows_b[...].reshape(2592, 128), column_shift(64)).astype(BF16)
    for d in range(18):
        for kh in range(3):
            first = 144 * d + 16 * (0, 5, 1)[kh]
            for kw in range(3):
                block = jnp.concatenate(
                    [
                        wide[first + 16 * j : first + 16 * j + 16, 128 * kw : 128 * kw + 128]
                        for j in range(4)
                    ],
                    axis=1,
                )
                cols[d, 16 * (3 * kh + kw) : 16 * (3 * kh + kw) + 16] = block
    for d in range(6):
        patch_b[d] = cols[d + 6]
    row = 2 * iy - 1 + lanes(128) // 32
    in_rows = jnp.logical_and(row >= 0, row < 32)
    acts = []
    for e in range(8):
        act = jnp.zeros((32, 512), F32)
        for d in (2 * e, 2 * e + 1):
            pre = dot(w_b, cols[d : d + 3].reshape(432, 512))
            if 4 <= d < 12:
                mask_b[d - 4] = jnp.where(pre > 0, 1.0, 0.0).astype(BF16)
            act = act + leaky(pre)
        acts.append(act)
    pool = dot_two(jnp.concatenate(acts, axis=0), second_pool())
    for e in range(8):
        deep = 2 * ix - 3 + e
        in_depth = jnp.logical_and(deep >= 0, deep < 2 * n_sx)
        out = pool[32 * e : 32 * e + 32]
        second[e] = jnp.where(jnp.logical_and(in_rows, in_depth), out, 0.0).astype(BF16)


def backward(
    n_sx, prev, own, nxt, got, mask_a, patch_a, mask_b, patch_b, w_second, taps,
    shift_c, shift_d, spread_b,
    parts, w_third, grads, cols_c, grads_c, cols_g, flip_c, flip_b, grads_b, cols_h, held,
):
    ix, iy = lax.axis_index("sx"), lax.axis_index("sy")
    arrived = got[...].astype(F32)
    for s in range(16):
        for g in range(7):
            w_third[4 * s : 4 * s + 4, 128 * g : 128 * g + 128] = arrived[s, 4 * g : 4 * g + 4]
        for j in range(3):
            grads[j, 4 * s : 4 * s + 4] = arrived[s, 28 + 4 * j : 32 + 4 * j]
    wide_w = w_third[...].astype(BF16)
    w_c = wide_w[:, 0:864]
    tall = jnp.concatenate([prev[...], own[...], nxt[...]], axis=2).reshape(256, 384)
    joined = dot(tall, brick_join()).astype(BF16)
    for k in range(9):
        shifted = dot(joined, shift_c[:, 256 * k : 256 * k + 256]).astype(BF16)
        for d in range(8):
            cols_c[d, 32 * k : 32 * k + 32] = shifted[32 * d : 32 * d + 32]
    row = lanes(256) // 32
    mine = jnp.logical_and(row >= 3, row < 5)
    spread_c = feature_spread()
    spreads = [dot(grads[j].astype(BF16), spread_c) for j in range(3)]
    pooled = jnp.zeros((64, 256), F32)
    third_wg = jnp.zeros((64, 864), F32)
    for e in range(1, 7):
        window = cols_c[e - 1 : e + 2].reshape(864, 256)
        pre = dot(w_c, window)
        back = (jnp.where(pre > 0, 1.0, SLOPE) * spreads[(e - 1) // 2]).astype(BF16)
        grads_c[e - 1] = back
        if e in (3, 4):
            pooled = pooled + leaky(pre)
            third_wg = third_wg + dot_t(jnp.where(mine, back, jnp.zeros((), BF16)), window)
    features = dot_two(pooled, third_pool())
    for k in range(9):
        shifted = dot(grads_c[...].reshape(384, 256), shift_c[:, 256 * k : 256 * k + 256])
        shifted = shifted.astype(BF16)
        for e in range(6):
            cols_g[e, 64 * k : 64 * k + 64] = shifted[64 * e : 64 * e + 64]
    for j in range(27):
        k = 26 - j
        flip_c[64 * j : 64 * j + 64, :] = w_third[:, 32 * k : 32 * k + 32]
    back_c = dot_t(unit(32, BF16), flip_c[...].astype(BF16)).astype(BF16)
    ups = [dot(back_c, cols_g[e : e + 3].reshape(1728, 256)) for e in range(4)]
    fine = dot_two(jnp.concatenate(ups, axis=0), spread_b[...])
    row = 4 * iy - 2 + lanes(512) // 64
    in_rows = jnp.logical_and(row >= 0, row < 64)
    row = lanes(512) // 64
    mine = jnp.logical_and(row >= 2, row < 6)
    second_wg = jnp.zeros((32, 432), F32)
    for d in range(1, 7):
        slope = jnp.where(mask_b[d].astype(F32) > 0.5, 1.0, SLOPE)
        deep = 4 * ix - 2 + d
        keep = jnp.logical_and(in_rows, jnp.logical_and(deep >= 0, deep < 4 * n_sx))
        back = jnp.where(keep, slope * fine[32 * (d // 2) : 32 * (d // 2) + 32], 0.0)
        if 2 <= d < 6:
            own_part = jnp.where(mine, back, 0.0).astype(BF16)
            second_wg = second_wg + dot_t(own_part, patch_b[d - 2 : d + 1].reshape(432, 512))
        grads_b[d - 1] = back.astype(BF16)
    for k in range(9):
        shifted = dot(grads_b[...].reshape(192, 512), shift_d[:, 256 * k : 256 * k + 256])
        shifted = shifted.astype(BF16)
        for d in range(6):
            cols_h[d, 32 * k : 32 * k + 32] = shifted[32 * d : 32 * d + 32]
    wb = w_second[...].astype(F32)
    for j in range(27):
        k = 26 - j
        flip_b[:, 32 * j : 32 * j + 32] = wb[16 * k : 16 * k + 16]
    back_b = flip_b[...][:, 0:864].astype(BF16)
    ups = [dot(back_b, cols_h[d : d + 3].reshape(864, 256)) for d in range(4)]
    left = lanes(128) < 64
    blocks = jnp.zeros((128, 256), F32)
    for d in range(4):
        one, two = (pltpu.roll(0.125 * ups[d][:, 128 * t : 128 * t + 128], 64, 1) for t in range(2))
        up = jnp.concatenate(
            [jnp.where(left, 0.0, one), jnp.where(left, one, two), jnp.where(left, two, 0.0)], axis=1
        )
        slope = jnp.where(mask_a[d].astype(F32) > 0.5, 1.0, SLOPE)
        back = (slope * jnp.concatenate([up] * 8, axis=0)).astype(BF16)
        blocks = blocks + dot_t(back, patch_a[d])
    first_wg = jnp.zeros((16, 128), F32)
    for p in range(8):
        first_wg = first_wg + dot_two(
            blocks[16 * p : 16 * p + 16], taps[256 * p : 256 * p + 256]
        )
    third_wg = jnp.concatenate([third_wg, jnp.zeros((64, 32), F32)], axis=1)
    second_wg = jnp.concatenate([second_wg, jnp.zeros((32, 80), F32)], axis=1)
    tails = third_wg[:, 768:896]
    early, late = pltpu.roll(features, 96, 1), pltpu.roll(features, 112, 1)
    second_tail, first_low = second_wg[:, 384:512], pltpu.roll(first_wg, 64, 1)
    for q in range(32):
        hi, s = divmod(q, 16)
        for j in range(2):
            o, f = 4 * s + 2 * hi + j, 4 * s + 2 * j
            for g in range(6):
                held[q, j : j + 1, 128 * g : 128 * g + 128] = third_wg[o : o + 1, 128 * g : 128 * g + 128]
            tail = tails[o : o + 1] + early[f : f + 1] + late[f + 1 : f + 2]
            held[q, j : j + 1, 768:896] = tail
        held[q, 0:1, 896:1024] = second_wg[q : q + 1, 0:128]
        held[q, 1:2, 896:1024] = second_wg[q : q + 1, 128:256]
        held[q, 0:1, 1024:1152] = second_wg[q : q + 1, 256:384]
        half = (first_low if hi == 0 else first_wg)[s : s + 1]
        held[q, 1:2, 1024:1152] = jnp.where(left, second_tail[q : q + 1], half)
    parts[...] = held[...].astype(BF16)


def summed(got):
    total = got[0].astype(F32)
    for s in range(1, got.shape[0]):
        total = total + got[s].astype(F32)
    return total


def spread_sum(got, total):
    out = summed(got).astype(BF16)
    for s in range(total.shape[0]):
        total[s] = out


def plane_sum(got, total, features, held):
    spread_sum(got, total)
    hi = lax.rem(lax.axis_index("sx"), 2)
    arrived = got[pl.ds(16 * hi, 16)].astype(F32)
    for o in range(4):
        for s in range(16):
            at = 864 + 16 * (o % 2)
            held[o, s : s + 1] = arrived[s, o // 2 : o // 2 + 1, at : at + 16]
    features[...] = held[...].astype(BF16)


def last(scale_a, scale_b, scale_c, got, first, second, third, held_a, held_b):
    held_a[...] = jnp.zeros(held_a.shape, F32)
    held_b[...] = jnp.zeros(held_b.shape, F32)
    for q in range(32):
        part = got[q].astype(F32)
        held_b[q : q + 1, 0:128] = part[0:1, 896:1024]
        held_b[q : q + 1, 128:256] = part[1:2, 896:1024]
        held_b[q : q + 1, 256:384] = part[0:1, 1024:1152]
        held_b[q : q + 1, 384:512] = part[1:2, 1024:1152]
    left = lanes(128) < 64
    low = pltpu.roll(held_b[0:16, 384:512], 64, 1)
    held_a[0:16] = jnp.where(left, low, held_b[16:32, 384:512])
    for hi in range(2):
        part = scale_c * got[16 * hi + lax.axis_index("sy")].astype(F32)
        for k in range(27):
            third[k, 2 * hi : 2 * hi + 2] = part[:, 32 * k : 32 * k + 32]
    turned_a = scale_a * jnp.transpose(held_a[...])
    for k in range(27):
        first[k] = turned_a[4 * k : 4 * k + 4, 0:16]
    for g in range(4):
        turned_b = scale_b * jnp.transpose(held_b[:, 128 * g : 128 * g + 128])
        for j in range(8):
            k = 8 * g + j
            if k < 27:
                second[k] = turned_b[16 * j : 16 * j + 16, 0:32]


def call(body, outs, scratch, *args, space=pltpu.VMEM, copies=0, limit=48 * 1024 * 1024, cost=1e8):
    semaphores = [pltpu.SemaphoreType.DMA((copies,))] if copies else []
    return pl.pallas_call(
        body,
        out_shape=[jax.ShapeDtypeStruct(shape, dtype) for shape, dtype in outs],
        in_specs=[pl.BlockSpec(memory_space=space)] * len(args),
        out_specs=[pl.BlockSpec(memory_space=pltpu.VMEM)] * len(outs),
        scratch_shapes=[pltpu.VMEM(shape, dtype) for shape, dtype in scratch] + semaphores,
        compiler_params=pltpu.CompilerParams(vmem_limit_bytes=limit),
        cost_estimate=pl.CostEstimate(flops=int(cost), bytes_accessed=10**5, transcendentals=0),
    )(*args)


def exchanged(to_prev, to_next, axis, step=1):
    ends = lax.axis_size(axis) - step
    from_prev = lax.ppermute(to_next, axis, [(i, i + step) for i in range(ends)])
    from_next = lax.ppermute(to_prev, axis, [(i + step, i) for i in range(ends)])
    return from_prev, from_next


def table(values, dtype=BF16):
    return jnp.asarray(values, dtype)


def shards(volume, w_first, w_second, w_third, feature_grad):
    n_sx, n_sy = lax.axis_size("sx"), lax.axis_size("sy")
    n_z = n_sx // 2
    cells = volume.shape[1] * volume.shape[2] * volume.shape[3] * n_sx * n_sy
    first_w = jnp.pad(w_first.transpose(2, 3, 4, 1, 0).reshape(108, 16), ((0, 20), (0, 0)))
    second_w = w_second.transpose(2, 3, 4, 1, 0).reshape(432, 32)
    third_w = w_third.transpose(2, 3, 4, 0, 1).reshape(27, 4, 32)
    taps = table(block_taps())

    (field,) = call(
        turned_field,
        [((11, 32, 128), BF16)],
        [((4, 8, 8, 128), BF16), ((4, 16, 16), BF16), ((27, 4, 32), BF16), ((96, 128), F32)],
        volume, feature_grad.reshape(4, 16, 16), third_w,
        space=pl.ANY, copies=3, limit=None,
    )
    prev, nxt = exchanged(field, field, "sx")
    far_prev, far_nxt = exchanged(field, field, "sx", 2)
    tall, sent = call(
        tall_field,
        [((38, 32, 128), BF16), ((16, 40, 128), BF16)],
        [((16, 40, 128), F32)],
        far_prev, prev, field, nxt, far_nxt,
    )
    got = lax.all_to_all(sent, "sy", 0, 0, tiled=True)
    prev, nxt = exchanged(tall, tall, "sy")
    field = jnp.concatenate([prev[:, 4:], tall, nxt, nxt[:, :4]], axis=1)
    field, got = lax.optimization_barrier((field, got))
    second, mask_a, patch_a, mask_b, patch_b = call(
        lambda *refs: forward(n_sx, *refs),
        [
            ((8, 32, 128), BF16), ((4, 128, 384), BF16), ((4, 256, 384), BF16),
            ((8, 32, 512), BF16), ((6, 144, 512), BF16),
        ],
        [((4, 38, 80, 128), BF16), ((18, 144, 128), BF16), ((18, 144, 512), BF16)],
        field, first_w, second_w, taps, cost=5e9,
    )
    prev, nxt = exchanged(second, second, "sy")
    (parts,) = call(
        lambda *refs: backward(n_sx, *refs),
        [((32, 2, 1152), BF16)],
        [
            ((64, 896), F32), ((3, 64, 128), F32), ((8, 288, 256), BF16), ((6, 64, 256), BF16),
            ((6, 576, 256), BF16), ((1728, 32), F32), ((16, 896), F32),
            ((6, 32, 512), BF16), ((6, 288, 256), BF16), ((32, 2, 1152), F32),
        ],
        prev, second, nxt, got, mask_a, patch_a, mask_b, patch_b, second_w, taps,
        table(tap_shift(8, 32, 0, 8)), table(tap_shift(8, 64, 2, 4)),
        table(second_spread()), cost=11e9,
    )
    planes = [[32 * z + i for i in range(32)] for z in range(n_z)]
    lines = [[2 * z + hi for z in range(n_z)] for hi in range(2)]
    both = ("sx", "sy")
    got = lax.all_to_all(parts, both, 0, 0, tiled=True, axis_index_groups=planes)
    total, features = call(
        plane_sum, [((n_z, 2, 1152), BF16), ((4, 16, 16), BF16)], [((4, 16, 16), F32)], got
    )
    got = lax.all_to_all(total, "sx", 0, 0, tiled=True, axis_index_groups=lines)
    (total,) = call(spread_sum, [((32, 2, 1152), BF16)], [], got)
    got = lax.all_to_all(total, both, 0, 0, tiled=True, axis_index_groups=planes)
    scales = (64.0 / math.sqrt(cells), 8.0 / math.sqrt(cells / 8), 1.0 / math.sqrt(cells / 64))
    first, second, third = call(
        lambda *refs: last(*scales, *refs),
        [((27, 4, 16), F32), ((27, 16, 32), F32), ((27, 4, 32), F32)],
        [((128, 128), F32), ((128, 512), F32)],
        got,
    )
    first_grad = first.reshape(3, 3, 3, 4, 16).transpose(4, 3, 0, 1, 2)
    second_grad = second.reshape(3, 3, 3, 16, 32).transpose(4, 3, 0, 1, 2)
    third_grad = third.reshape(3, 3, 3, 4, 32).transpose(3, 4, 0, 1, 2)
    return (features.reshape(4, 1, 16, 16), first_grad, second_grad, third_grad)


def solution(mesh):
    in_specs = (
        P(None, "sx", "sy", None),
        P(),
        P(),
        P("sy", None, None, None, None),
        P("sy", "sx", None, None),
    )
    out_specs = (P("sy", "sx", None, None), P(), P(), P("sy", None, None, None, None))
    return jax.shard_map(shards, mesh=mesh, in_specs=in_specs, out_specs=out_specs, check_vma=False)
```

```python
import math

import jax
import jax.numpy as jnp
import numpy as np
from jax import lax
from jax.experimental import pallas as pl
from jax.experimental.pallas import tpu as pltpu
from jax.sharding import PartitionSpec as P

SLOPE = 0.3
BF16 = jnp.bfloat16
F32 = jnp.float32


def tap_shift(rows, cols, out_first, out_rows):
    table = np.zeros((rows, cols, 3, 3, out_rows, cols), np.float32)
    for kh in range(3):
        for kw in range(3):
            for r in range(out_rows):
                for w in range(cols):
                    row, col = out_first + r + kh - 1, w + kw - 1
                    if 0 <= row < rows and 0 <= col < cols:
                        table[row, col, kh, kw, r, w] = 1
    return table.reshape(rows * cols, 9 * out_rows * cols)


def second_spread():
    table = np.zeros((8, 32, 8, 64), np.float32)
    for r in range(8):
        for w in range(64):
            table[2 + r // 2, w // 2, r, w] = 0.125
    return table.reshape(256, 512)


def block_taps():
    table = np.zeros((2, 2, 2, 4, 4, 4, 4, 128), np.float32)
    for pd, ph, pw in np.ndindex(2, 2, 2):
        for kd, kh, kw, c in np.ndindex(3, 3, 3, 4):
            at = ((kd * 3 + kh) * 3 + kw) * 4 + c
            table[pd, ph, pw, kd + pd, kw + pw, kh + ph, c, at] = 1
    return table.reshape(2048, 128)


def dot(a, b):
    return lax.dot_general(a, b, (((1,), (0,)), ((), ())), preferred_element_type=F32)


def dot_t(a, b):
    return lax.dot_general(a, b, (((1,), (1,)), ((), ())), preferred_element_type=F32)


def placed(shape, match, value=1.0, dtype=BF16):
    row, lane = (lax.broadcasted_iota(jnp.int32, shape, axis) for axis in range(2))
    return jnp.where(match(row, lane), value, 0.0).astype(dtype)


def unit(size, dtype):
    return placed((size, size), lambda row, lane: row == lane, 1.0, dtype)


def turned():
    return placed((32, 32), lambda row, lane: lane == (row & 3) * 8 + (row >> 2))


def column_shift(cols):
    def match(row, lane):
        to = (lane & 127) + (lane >> 7) - 1
        return jnp.logical_and(row == to, (row // cols) == (lane & 127) // cols)

    return placed((128, 384), match)


def column_pairs():
    return placed((128, 512), lambda row, lane: row == 2 * (lane & 63) + (lane >> 7) - 1)


def second_pool():
    return placed((512, 128), lambda row, lane: lane == (row >> 7) * 32 + ((row & 63) >> 1), 0.125)


def third_pool():
    def match(row, lane):
        inside = jnp.logical_and(row >= 96, row < 160)
        return jnp.logical_and(inside, lane == ((row & 31) >> 1))

    return placed((256, 128), match, 0.125)


def feature_spread():
    def match(row, lane):
        inside = jnp.logical_and(lane >= 32, lane < 224)
        return jnp.logical_and(inside, row == ((lane - 32) >> 6) * 16 + ((lane & 31) >> 1))

    return placed((128, 256), match, 0.125)


def brick_join():
    def match(row, lane):
        return row == lane + jnp.where(lane < 64, 0, jnp.where(lane < 192, 64, 128))

    return placed((384, 256), match)


def dot_two(a, b):
    high = a.astype(BF16)
    low = (a - high.astype(F32)).astype(BF16)
    out = dot(jnp.concatenate([high, low], axis=0), b)
    return out[: a.shape[0]] + out[a.shape[0] :]


def leaky(values):
    return jnp.where(values > 0, values, SLOPE * values)


def lanes(count):
    return lax.broadcasted_iota(jnp.int32, (1, count), 1)


def turned_field(volume_in, grads_in, weights_in, field, volume, feature_grad, w_third, held, done):
    pairs = ((volume_in, volume), (grads_in, feature_grad), (weights_in, w_third))
    copies = [pltpu.make_async_copy(a, b, done.at[i]) for i, (a, b) in enumerate(pairs)]
    for copy in copies:
        copy.start()
    held[...] = jnp.zeros(held.shape, F32)
    turn = turned()
    copies[1].wait()
    grads = feature_grad[...].astype(F32)
    for s in range(16):
        for i in range(3):
            h = s + i - 1
            if 0 <= h < 16:
                held[4 * s : 4 * s + 4, 16 * i : 16 * i + 16] = grads[:, h, :]
    copies[2].wait()
    for k in range(27):
        g, i = divmod(k, 4)
        held[64 + 4 * g : 68 + 4 * g, 32 * i : 32 * i + 32] = w_third[k].astype(F32)
    for t in range(3):
        field[8 + t] = held[32 * t : 32 * t + 32].astype(BF16)
    copies[0].wait()
    for d in range(8):
        stack = jnp.concatenate([volume[c, d].astype(F32) for c in range(4)], axis=0)
        field[d] = dot(turn, stack.astype(BF16)).astype(BF16)


def tall_field(far_prev, prev, own, nxt, far_nxt, tall, sent, held):
    for d in range(7):
        tall[d] = far_prev[d + 1]
        tall[31 + d] = far_nxt[d]
    for d in range(8):
        tall[7 + d] = prev[d]
        tall[15 + d] = own[d]
        tall[23 + d] = nxt[d]
    weights = own[10].astype(F32)[0:28]
    for s in range(16):
        held[s, 0:28] = weights
    for j, part in enumerate((prev, own, nxt)):
        for t in range(2):
            grads = part[8 + t].astype(F32)
            for s in range(8):
                held[8 * t + s, 28 + 4 * j : 32 + 4 * j] = grads[4 * s : 4 * s + 4]
    sent[...] = held[...].astype(BF16)


def forward_weights(w_first, w_second, taps, w_a, w_b):
    turned_w = dot_t(unit(16, BF16), w_first[...]).astype(BF16)
    w_a[...] = jnp.concatenate(
        [dot_t(turned_w, taps[256 * p : 256 * p + 256]).astype(BF16) for p in range(8)], axis=0
    )
    w_b[...] = dot_t(unit(32, BF16), w_second[...]).astype(BF16)


def backward_weights(got, w_second, w_c, spreads, back_c, back_b, w_third, grads, flip_c, flip_b):
    arrived = got[...].astype(F32)
    for s in range(16):
        for g in range(7):
            w_third[4 * s : 4 * s + 4, 128 * g : 128 * g + 128] = arrived[s, 4 * g : 4 * g + 4]
        for j in range(3):
            grads[j, 4 * s : 4 * s + 4] = arrived[s, 28 + 4 * j : 32 + 4 * j]
    w_c[...] = w_third[...].astype(BF16)
    spread_c = feature_spread()
    for j in range(3):
        spreads[j] = dot(grads[j].astype(BF16), spread_c)
    for j in range(27):
        k = 26 - j
        flip_c[64 * j : 64 * j + 64, :] = w_third[:, 32 * k : 32 * k + 32]
    back_c[...] = dot_t(unit(32, BF16), flip_c[...].astype(BF16)).astype(BF16)
    wb = w_second[...].astype(F32)
    for j in range(27):
        k = 26 - j
        flip_b[:, 32 * j : 32 * j + 32] = wb[16 * k : 16 * k + 16]
    back_b[...] = flip_b[...][:, 0:864].astype(BF16)


def forward(
    n_sx, field, w_a, w_b,
    second, mask_a, patch_a, mask_b, patch_b, cells, rows_b, cols,
):
    ix, iy = lax.axis_index("sx"), lax.axis_index("sy")
    left = lanes(128) < 64
    flat = field[...].reshape(3648, 128)
    pairs = column_pairs()
    for half in range(2):
        wide = dot(flat, pairs[:, 256 * half : 256 * half + 256])
        for t in range(2):
            for d in range(38):
                part = wide[96 * d : 96 * d + 96, 128 * t : 128 * t + 128]
                cells[2 * half + t, d] = jnp.where(left, part[0:80], part[8:88]).astype(BF16)
    pair = lanes(128) // 64
    for two in range(9):
        rows = []
        for kd in range(4):
            for t in range(4):
                pieces = []
                for d in (2 * two, 2 * two + 1):
                    for a in range(5):
                        pieces.append(cells[t, 2 * d + kd, 16 * a : 16 * a + 16])
                rows.append(jnp.concatenate(pieces, axis=1))
        patch = jnp.concatenate(rows, axis=0)
        pre = dot(w_a[...], patch)
        act = leaky(pre)
        pool = act[0:16]
        for p in range(1, 8):
            pool = pool + act[16 * p : 16 * p + 16]
        pool = 0.125 * pool
        for t in range(2):
            d = 2 * two + t
            start = 640 * t
            if 7 <= d < 11:
                own = pre[:, start + 128 : start + 512]
                mask_a[d - 7] = jnp.where(own > 0, 1.0, 0.0).astype(BF16)
                patch_a[d - 7] = patch[:, start + 128 : start + 512]
            deep = 4 * ix - 7 + d
            in_depth = jnp.logical_and(deep >= 0, deep < 4 * n_sx)
            kept = []
            for a in range(5):
                row = 4 * iy - 3 + 2 * a + pair
                keep = jnp.logical_and(jnp.logical_and(row >= 0, row < 64), in_depth)
                kept.append(jnp.where(keep, pool[:, start + 128 * a : start + 128 * a + 128], 0.0))
            kept = jnp.concatenate(kept, axis=0)
            swapped = pltpu.roll(kept, 64, 1)
            odd = jnp.where(left, swapped[0:64], swapped[16:80])
            rows_b[d] = jnp.concatenate([kept, odd], axis=0).astype(BF16)
    wide = dot(rows_b[...].reshape(2592, 128), column_shift(64)).astype(BF16)
    for d in range(18):
        for kh in range(3):
            first = 144 * d + 16 * (0, 5, 1)[kh]
            for kw in range(3):
                block = jnp.concatenate(
                    [
                        wide[first + 16 * j : first + 16 * j + 16, 128 * kw : 128 * kw + 128]
                        for j in range(4)
                    ],
                    axis=1,
                )
                cols[d, 16 * (3 * kh + kw) : 16 * (3 * kh + kw) + 16] = block
    for d in range(6):
        patch_b[d] = cols[d + 6]
    row = 2 * iy - 1 + lanes(128) // 32
    in_rows = jnp.logical_and(row >= 0, row < 32)
    acts = []
    for e in range(8):
        act = jnp.zeros((32, 512), F32)
        for d in (2 * e, 2 * e + 1):
            pre = dot(w_b[...], cols[d : d + 3].reshape(432, 512))
            if 4 <= d < 12:
                mask_b[d - 4] = jnp.where(pre > 0, 1.0, 0.0).astype(BF16)
            act = act + leaky(pre)
        acts.append(act)
    pool = dot_two(jnp.concatenate(acts, axis=0), second_pool())
    for e in range(8):
        deep = 2 * ix - 3 + e
        in_depth = jnp.logical_and(deep >= 0, deep < 2 * n_sx)
        out = pool[32 * e : 32 * e + 32]
        second[e] = jnp.where(jnp.logical_and(in_rows, in_depth), out, 0.0).astype(BF16)


def backward(
    n_sx, prev, own, nxt, w_c, spreads, back_c, back_b, mask_a, patch_a, mask_b, patch_b, taps,
    shift_c, shift_d, spread_b,
    parts, cols_c, grads_c, cols_g, grads_b, cols_h, held,
):
    ix, iy = lax.axis_index("sx"), lax.axis_index("sy")
    tall = jnp.concatenate([prev[...], own[...], nxt[...]], axis=2).reshape(256, 384)
    joined = dot(tall, brick_join()).astype(BF16)
    for k in range(9):
        shifted = dot(joined, shift_c[:, 256 * k : 256 * k + 256]).astype(BF16)
        for d in range(8):
            cols_c[d, 32 * k : 32 * k + 32] = shifted[32 * d : 32 * d + 32]
    row = lanes(256) // 32
    mine = jnp.logical_and(row >= 3, row < 5)
    pooled = jnp.zeros((64, 256), F32)
    third_wg = jnp.zeros((64, 864), F32)
    for e in range(1, 7):
        window = cols_c[e - 1 : e + 2].reshape(864, 256)
        pre = dot(w_c[:, 0:864], window)
        back = (jnp.where(pre > 0, 1.0, SLOPE) * spreads[(e - 1) // 2]).astype(BF16)
        grads_c[e - 1] = back
        if e in (3, 4):
            pooled = pooled + leaky(pre)
            third_wg = third_wg + dot_t(jnp.where(mine, back, jnp.zeros((), BF16)), window)
    features = dot_two(pooled, third_pool())
    for k in range(9):
        shifted = dot(grads_c[...].reshape(384, 256), shift_c[:, 256 * k : 256 * k + 256])
        shifted = shifted.astype(BF16)
        for e in range(6):
            cols_g[e, 64 * k : 64 * k + 64] = shifted[64 * e : 64 * e + 64]
    ups = [dot(back_c[...], cols_g[e : e + 3].reshape(1728, 256)) for e in range(4)]
    fine = dot_two(jnp.concatenate(ups, axis=0), spread_b[...])
    row = 4 * iy - 2 + lanes(512) // 64
    in_rows = jnp.logical_and(row >= 0, row < 64)
    row = lanes(512) // 64
    mine = jnp.logical_and(row >= 2, row < 6)
    second_wg = jnp.zeros((32, 432), F32)
    for d in range(1, 7):
        slope = jnp.where(mask_b[d].astype(F32) > 0.5, 1.0, SLOPE)
        deep = 4 * ix - 2 + d
        keep = jnp.logical_and(in_rows, jnp.logical_and(deep >= 0, deep < 4 * n_sx))
        back = jnp.where(keep, slope * fine[32 * (d // 2) : 32 * (d // 2) + 32], 0.0)
        if 2 <= d < 6:
            own_part = jnp.where(mine, back, 0.0).astype(BF16)
            second_wg = second_wg + dot_t(own_part, patch_b[d - 2 : d + 1].reshape(432, 512))
        grads_b[d - 1] = back.astype(BF16)
    for k in range(9):
        shifted = dot(grads_b[...].reshape(192, 512), shift_d[:, 256 * k : 256 * k + 256])
        shifted = shifted.astype(BF16)
        for d in range(6):
            cols_h[d, 32 * k : 32 * k + 32] = shifted[32 * d : 32 * d + 32]
    ups = [dot(back_b[...], cols_h[d : d + 3].reshape(864, 256)) for d in range(4)]
    left = lanes(128) < 64
    blocks = jnp.zeros((128, 256), F32)
    for d in range(4):
        one, two = (pltpu.roll(0.125 * ups[d][:, 128 * t : 128 * t + 128], 64, 1) for t in range(2))
        up = jnp.concatenate(
            [jnp.where(left, 0.0, one), jnp.where(left, one, two), jnp.where(left, two, 0.0)], axis=1
        )
        slope = jnp.where(mask_a[d].astype(F32) > 0.5, 1.0, SLOPE)
        back = (slope * jnp.concatenate([up] * 8, axis=0)).astype(BF16)
        blocks = blocks + dot_t(back, patch_a[d])
    first_wg = jnp.zeros((16, 128), F32)
    for p in range(8):
        first_wg = first_wg + dot_two(
            blocks[16 * p : 16 * p + 16], taps[256 * p : 256 * p + 256]
        )
    third_wg = jnp.concatenate([third_wg, jnp.zeros((64, 32), F32)], axis=1)
    second_wg = jnp.concatenate([second_wg, jnp.zeros((32, 80), F32)], axis=1)
    tails = third_wg[:, 768:896]
    early, late = pltpu.roll(features, 96, 1), pltpu.roll(features, 112, 1)
    second_tail, first_low = second_wg[:, 384:512], pltpu.roll(first_wg, 64, 1)
    for q in range(32):
        hi, s = divmod(q, 16)
        for j in range(2):
            o, f = 4 * s + 2 * hi + j, 4 * s + 2 * j
            for g in range(6):
                held[q, j : j + 1, 128 * g : 128 * g + 128] = third_wg[o : o + 1, 128 * g : 128 * g + 128]
            tail = tails[o : o + 1] + early[f : f + 1] + late[f + 1 : f + 2]
            held[q, j : j + 1, 768:896] = tail
        held[q, 0:1, 896:1024] = second_wg[q : q + 1, 0:128]
        held[q, 1:2, 896:1024] = second_wg[q : q + 1, 128:256]
        held[q, 0:1, 1024:1152] = second_wg[q : q + 1, 256:384]
        half = (first_low if hi == 0 else first_wg)[s : s + 1]
        held[q, 1:2, 1024:1152] = jnp.where(left, second_tail[q : q + 1], half)
    parts[...] = held[...].astype(BF16)


def summed(got):
    total = got[0].astype(F32)
    for s in range(1, got.shape[0]):
        total = total + got[s].astype(F32)
    return total


def spread_sum(got, total):
    out = summed(got).astype(BF16)
    for s in range(total.shape[0]):
        total[s] = out


def plane_sum(got, total, features, held):
    spread_sum(got, total)
    hi = lax.rem(lax.axis_index("sx"), 2)
    arrived = got[pl.ds(16 * hi, 16)].astype(F32)
    for o in range(4):
        for s in range(16):
            at = 864 + 16 * (o % 2)
            held[o, s : s + 1] = arrived[s, o // 2 : o // 2 + 1, at : at + 16]
    features[...] = held[...].astype(BF16)


def last(scale_a, scale_b, scale_c, got, first, second, third, held_a, held_b):
    held_a[...] = jnp.zeros(held_a.shape, F32)
    held_b[...] = jnp.zeros(held_b.shape, F32)
    for q in range(32):
        part = got[q].astype(F32)
        held_b[q : q + 1, 0:128] = part[0:1, 896:1024]
        held_b[q : q + 1, 128:256] = part[1:2, 896:1024]
        held_b[q : q + 1, 256:384] = part[0:1, 1024:1152]
        held_b[q : q + 1, 384:512] = part[1:2, 1024:1152]
    left = lanes(128) < 64
    low = pltpu.roll(held_b[0:16, 384:512], 64, 1)
    held_a[0:16] = jnp.where(left, low, held_b[16:32, 384:512])
    for hi in range(2):
        part = scale_c * got[16 * hi + lax.axis_index("sy")].astype(F32)
        for k in range(27):
            third[k, 2 * hi : 2 * hi + 2] = part[:, 32 * k : 32 * k + 32]
    turned_a = scale_a * jnp.transpose(held_a[...])
    for k in range(27):
        first[k] = turned_a[4 * k : 4 * k + 4, 0:16]
    for g in range(4):
        turned_b = scale_b * jnp.transpose(held_b[:, 128 * g : 128 * g + 128])
        for j in range(8):
            k = 8 * g + j
            if k < 27:
                second[k] = turned_b[16 * j : 16 * j + 16, 0:32]


def call(body, outs, scratch, *args, space=pltpu.VMEM, copies=0, limit=48 * 1024 * 1024, cost=1e8):
    semaphores = [pltpu.SemaphoreType.DMA((copies,))] if copies else []
    return pl.pallas_call(
        body,
        out_shape=[jax.ShapeDtypeStruct(shape, dtype) for shape, dtype in outs],
        in_specs=[pl.BlockSpec(memory_space=space)] * len(args),
        out_specs=[pl.BlockSpec(memory_space=pltpu.VMEM)] * len(outs),
        scratch_shapes=[pltpu.VMEM(shape, dtype) for shape, dtype in scratch] + semaphores,
        compiler_params=pltpu.CompilerParams(vmem_limit_bytes=limit),
        cost_estimate=pl.CostEstimate(flops=int(cost), bytes_accessed=10**5, transcendentals=0),
    )(*args)


def exchanged(to_prev, to_next, axis, step=1):
    ends = lax.axis_size(axis) - step
    from_prev = lax.ppermute(to_next, axis, [(i, i + step) for i in range(ends)])
    from_next = lax.ppermute(to_prev, axis, [(i + step, i) for i in range(ends)])
    return from_prev, from_next


def table(values, dtype=BF16):
    return jnp.asarray(values, dtype)


def shards(volume, w_first, w_second, w_third, feature_grad):
    n_sx, n_sy = lax.axis_size("sx"), lax.axis_size("sy")
    n_z = n_sx // 2
    cells = volume.shape[1] * volume.shape[2] * volume.shape[3] * n_sx * n_sy
    first_w = jnp.pad(w_first.transpose(2, 3, 4, 1, 0).reshape(108, 16), ((0, 20), (0, 0)))
    second_w = w_second.transpose(2, 3, 4, 1, 0).reshape(432, 32)
    third_w = w_third.transpose(2, 3, 4, 0, 1).reshape(27, 4, 32)
    taps = table(block_taps())

    (field,) = call(
        turned_field,
        [((11, 32, 128), BF16)],
        [((4, 8, 8, 128), BF16), ((4, 16, 16), BF16), ((27, 4, 32), BF16), ((96, 128), F32)],
        volume, feature_grad.reshape(4, 16, 16), third_w,
        space=pl.ANY, copies=3, limit=None,
    )
    prev, nxt = exchanged(field, field, "sx")
    far_prev, far_nxt = exchanged(field, field, "sx", 2)
    tall, sent = call(
        tall_field,
        [((38, 32, 128), BF16), ((16, 40, 128), BF16)],
        [((16, 40, 128), F32)],
        far_prev, prev, field, nxt, far_nxt,
    )
    got = lax.all_to_all(sent, "sy", 0, 0, tiled=True)
    prev, nxt = exchanged(tall, tall, "sy")
    field = jnp.concatenate([prev[:, 4:], tall, nxt, nxt[:, :4]], axis=1)
    field, got = lax.optimization_barrier((field, got))
    w_a, w_b = call(
        forward_weights,
        [((128, 256), BF16), ((32, 432), BF16)], [], first_w, second_w, taps, cost=5e8,
    )
    second, mask_a, patch_a, mask_b, patch_b = call(
        lambda *refs: forward(n_sx, *refs),
        [
            ((8, 32, 128), BF16), ((4, 128, 384), BF16), ((4, 256, 384), BF16),
            ((8, 32, 512), BF16), ((6, 144, 512), BF16),
        ],
        [((4, 38, 80, 128), BF16), ((18, 144, 128), BF16), ((18, 144, 512), BF16)],
        field, w_a, w_b, cost=5e9,
    )
    prev, nxt = exchanged(second, second, "sy")
    w_c, spreads, back_c, back_b = call(
        backward_weights,
        [((64, 896), BF16), ((3, 64, 256), F32), ((32, 1728), BF16), ((16, 864), BF16)],
        [((64, 896), F32), ((3, 64, 128), F32), ((1728, 32), F32), ((16, 896), F32)],
        got, second_w, cost=15e8,
    )
    (parts,) = call(
        lambda *refs: backward(n_sx, *refs),
        [((32, 2, 1152), BF16)],
        [
            ((8, 288, 256), BF16), ((6, 64, 256), BF16),
            ((6, 576, 256), BF16),
            ((6, 32, 512), BF16), ((6, 288, 256), BF16), ((32, 2, 1152), F32),
        ],
        prev, second, nxt, w_c, spreads, back_c, back_b, mask_a, patch_a, mask_b, patch_b, taps,
        table(tap_shift(8, 32, 0, 8)), table(tap_shift(8, 64, 2, 4)),
        table(second_spread()), cost=11e9,
    )
    planes = [[32 * z + i for i in range(32)] for z in range(n_z)]
    lines = [[2 * z + hi for z in range(n_z)] for hi in range(2)]
    both = ("sx", "sy")
    got = lax.all_to_all(parts, both, 0, 0, tiled=True, axis_index_groups=planes)
    total, features = call(
        plane_sum, [((n_z, 2, 1152), BF16), ((4, 16, 16), BF16)], [((4, 16, 16), F32)], got
    )
    got = lax.all_to_all(total, "sx", 0, 0, tiled=True, axis_index_groups=lines)
    (total,) = call(spread_sum, [((32, 2, 1152), BF16)], [], got)
    got = lax.all_to_all(total, both, 0, 0, tiled=True, axis_index_groups=planes)
    scales = (64.0 / math.sqrt(cells), 8.0 / math.sqrt(cells / 8), 1.0 / math.sqrt(cells / 64))
    first, second, third = call(
        lambda *refs: last(*scales, *refs),
        [((27, 4, 16), F32), ((27, 16, 32), F32), ((27, 4, 32), F32)],
        [((128, 128), F32), ((128, 512), F32)],
        got,
    )
    first_grad = first.reshape(3, 3, 3, 4, 16).transpose(4, 3, 0, 1, 2)
    second_grad = second.reshape(3, 3, 3, 16, 32).transpose(4, 3, 0, 1, 2)
    third_grad = third.reshape(3, 3, 3, 4, 32).transpose(3, 4, 0, 1, 2)
    return (features.reshape(4, 1, 16, 16), first_grad, second_grad, third_grad)


def solution(mesh):
    in_specs = (
        P(None, "sx", "sy", None),
        P(),
        P(),
        P("sy", None, None, None, None),
        P("sy", "sx", None, None),
    )
    out_specs = (P("sy", "sx", None, None), P(), P(), P("sy", None, None, None, None))
    return jax.shard_map(shards, mesh=mesh, in_specs=in_specs, out_specs=out_specs, check_vma=False)
```
